128 devices in a mesh: row: 64 (over z, y_lo, x, core), col: 2 (over y_hi).
Axes of the slice: x: 4, y: 4 (y_hi: 2, y_lo: 2; y = y_hi * 2 + y_lo), z: 4, core: 2. Of those that a mesh axis runs over, the one named last changes fastest.
Arguments:
- front_matrix: float32 [16384, 16384], P('row', 'col'), may hold values from -0.35 to 8.35, as said below
- row_map: int32 [64, 256], P('row'), may hold values from 0 to 16383, as said below
Outputs:
- factor_panels: float32 [16384, 768], P('row')
- parent_rows: float32 [16384, 16384], P('row', 'col')
The draws below stay inside these ranges and needn't reach their ends.
Inputs may be any that keep to these rules, and one draw needn't show every extreme that they name: `row_map`: the rows of all blocks name every parent row exactly once. The 256 rows of one block go in runs of exactly 4 consecutive rows, each run to a different parent row block of 256 rows. `front_matrix`: Symmetric; its leading 3 * 256 x 3 * 256 block is positive definite.
All inputs are finite; a program needn't handle non-finite values.
Results may differ from the reference program's by a relative error of at most 0.0001.
Values sent between devices are 32-bit elements; how exact they have to be, the bound alone decides.
No kernel may reach another device: no remote copies, remote signals or barrier semaphores. Data moves between devices by JAX's collectives and lax.ppermute only.
A program may use at most 128 MiB of HBM per device.

```python
import jax
import jax.numpy as jnp
from jax import lax

BW = 128
NP = 3
PW = 256
F = 16384
CAP = 4
N_ROW = 64
N_COL = 2


def draw_front_matrix(key, part):
    base_key = jax.random.fold_in(key, 3)
    noise_key, diag_key = jax.random.split(base_key)
    noise = jnp.clip(jax.random.normal(noise_key, (F, F), jnp.float32), -6.0, 6.0)
    symmetric = (noise + noise.T) * (0.04 * 0.70710678)
    diag_values = jnp.exp(jax.random.uniform(diag_key, (F,), jnp.float32, jnp.log(3.0), jnp.log(8.0)))
    row_ids = lax.broadcasted_iota(jnp.int32, (F, F), 0)
    col_ids = lax.broadcasted_iota(jnp.int32, (F, F), 1)
    logical = jnp.where(row_ids == col_ids, symmetric + diag_values[:, None], symmetric)
    return logical.reshape(F, N_ROW, N_COL, BW).transpose(0, 2, 1, 3).reshape(F, F)


def permute_lanes(lane_key):
    return jax.random.permutation(lane_key, PW)


def draw_row_map(key, part):
    base_key = jax.random.fold_in(key, 7)
    keys = jax.random.split(base_key, 4)
    first_perm = jax.random.permutation(keys[0], N_ROW)
    second_perm = jax.random.permutation(keys[1], N_ROW)
    offsets = jax.random.permutation(keys[2], N_ROW)
    positions = jax.vmap(permute_lanes)(jax.random.split(keys[3], N_ROW))
    lanes = jnp.arange(PW, dtype=jnp.int32)
    groups = lanes // CAP
    target = second_perm[(first_perm[:, None] + offsets[groups][None, :]) % N_ROW]
    local_rows = positions[target, lanes[None, :]]
    return (target * PW + local_rows).astype(jnp.int32)


def setup_inputs(seed: int = 0) -> dict:
    splits = jax.random.split(jax.random.key(seed), 3)
    return {
        "front_matrix": draw_front_matrix(jax.random.fold_in(splits[2], 71), 0),
        "row_map": draw_row_map(jax.random.fold_in(splits[2], 71), 0),
    }


exact_prec = lax.Precision.HIGHEST

def to_logical(matrix):
    order = matrix.shape[0]
    return matrix.reshape(order, N_COL, N_ROW, BW).transpose(0, 2, 1, 3).reshape(order, order)

def to_stored(matrix):
    order = matrix.shape[0]
    return matrix.reshape(order, N_ROW, N_COL, BW).transpose(0, 2, 1, 3).reshape(order, order)

def reference(front_matrix, row_map):
    working = to_logical(front_matrix)
    order = working.shape[0]
    width_panel = BW * N_COL
    row_ids = jnp.arange(order, dtype=jnp.int32)
    panels = []
    for step_index in range(NP):
        low_edge = step_index * width_panel
        diagonal = working[low_edge:low_edge + width_panel, low_edge:low_edge + width_panel]
        lower_factor = jnp.linalg.cholesky(diagonal)
        identity = jnp.eye(width_panel, dtype=working.dtype)
        inverse = lax.linalg.triangular_solve(lower_factor, identity, left_side=True, lower=True)
        current = jnp.dot(working[:, low_edge:low_edge + width_panel], inverse.T, precision=exact_prec)
        current = jnp.where((row_ids >= low_edge)[:, None], current, 0.0)
        working = working - jnp.dot(current, current.T, precision=exact_prec)
        panels.append(current)
    keep_ids = row_ids >= NP * width_panel
    contribution = jnp.where(keep_ids[:, None] & keep_ids[None, :], working, 0.0)
    assembled = jnp.zeros_like(contribution).at[row_map.reshape(-1)].add(contribution)
    return (jnp.concatenate(panels, axis=1), to_stored(assembled))
```

```python
import jax
import jax.numpy as jnp
from jax import lax
from jax.experimental import pallas as pl
from jax.experimental.pallas import tpu as pltpu
from jax.sharding import PartitionSpec as P

NP = 3
N_ROW = 64
CAP = 4
PW = 256

full = lax.Precision.HIGHEST


def dot_t(a, b):
    return lax.dot_general(
        a, b, (((1,), (1,)), ((), ())), precision=full, preferred_element_type=jnp.float32
    )


def dot_n(a, b):
    return lax.dot_general(
        a, b, (((1,), (0,)), ((), ())), precision=full, preferred_element_type=jnp.float32
    )


def row_id(z, y, x, k):
    return ((z * 2 + y) * 4 + x) * 2 + k


def spread(block, root):
    row = lax.axis_index("row")
    sizes = (4, 2, 4, 2)
    strides = (16, 8, 2, 1)
    start = tuple((root // s) % n for s, n in zip(strides, sizes))
    have = [start]
    value = block
    for axis in (2, 0, 1, 3):
        got = value
        for step in range(1, sizes[axis]):
            pairs = []
            for h in have:
                to = list(h)
                to[axis] = (h[axis] + step) % sizes[axis]
                pairs.append((row_id(*h), row_id(*to)))
            arrived = lax.ppermute(value, "row", pairs)
            mine = (row // strides[axis]) % sizes[axis]
            got = jnp.where(mine == (start[axis] + step) % sizes[axis], arrived, got)
        value = got
        more = []
        for h in have:
            for step in range(sizes[axis]):
                to = list(h)
                to[axis] = (h[axis] + step) % sizes[axis]
                more.append(tuple(to))
        have = more
    return value


def pack_kernel(slot_ref, rows_ref, out_ref):
    for g in range(N_ROW):
        out_ref[slot_ref[g]] = rows_ref[g * CAP : (g + 1) * CAP, :]


def pack_runs(slots, rows, tile=512):
    height, width = rows.shape
    return pl.pallas_call(
        pack_kernel,
        out_shape=jax.ShapeDtypeStruct((N_ROW, CAP, width), rows.dtype),
        grid_spec=pltpu.PrefetchScalarGridSpec(
            num_scalar_prefetch=1,
            grid=(width // tile,),
            in_specs=[pl.BlockSpec((height, tile), lambda i, s: (0, i))],
            out_specs=pl.BlockSpec((N_ROW, CAP, tile), lambda i, s: (0, 0, i)),
        ),
        cost_estimate=pl.CostEstimate(
            flops=0, bytes_accessed=2 * 4 * height * width, transcendentals=0
        ),
        name="pack_runs",
    )(slots, rows)


def inverse_factor(block):
    lower = jnp.linalg.cholesky(block)
    eye = jnp.eye(PW, dtype=jnp.float32)
    return lax.linalg.triangular_solve(lower, eye, left_side=True, lower=True)


def panel_rows(rows, w0, w1, w2, l10, l20, l21):
    a0, a1, a2 = rows[:, :PW], rows[:, PW : 2 * PW], rows[:, 2 * PW :]
    l0 = dot_t(a0, w0)
    l1 = dot_t(a1 - dot_t(l0, l10), w1)
    l2 = dot_t(a2 - dot_t(l0, l20) - dot_t(l1, l21), w2)
    return l0, l1, l2


def weave(own, other, col):
    first = jnp.where(col == 0, own, other)
    second = jnp.where(col == 0, other, own)
    parts = []
    for k in range(NP):
        parts += [first[:, k * 128 : (k + 1) * 128], second[:, k * 128 : (k + 1) * 128]]
    return jnp.concatenate(parts, axis=1)


def local(front_matrix, row_map):
    width = front_matrix.shape[1]
    row = lax.axis_index("row")
    col = lax.axis_index("col")
    swap = [(0, 1), (1, 0)]
    head = NP * 128
    own = front_matrix[:, :head]
    panel = weave(own, lax.ppermute(own, "col", swap), col)

    targets = row_map[0].reshape(N_ROW, CAP)[:, 0] // PW
    within = (row_map[0] % PW).reshape(N_ROW, CAP)
    hits = targets[None, :] == jnp.arange(N_ROW, dtype=jnp.int32)[:, None]
    outgoing = pack_runs(targets, front_matrix)
    out_index = jnp.sum(jnp.where(hits[:, :, None], within[None, :, :], 0), axis=1)
    arrived_index = lax.all_to_all(out_index, "row", split_axis=0, concat_axis=0, tiled=True)
    arrived = lax.all_to_all(outgoing, "row", split_axis=0, concat_axis=0, tiled=True)

    mine = lax.dynamic_slice_in_dim(panel, col * 128, 128, 0)
    gathered = lax.all_gather(mine, "row", axis=0, tiled=True)

    s0 = spread(panel[:, :PW], 0)
    s1 = spread(panel[:, : 2 * PW], 1)
    s2 = spread(panel, 2)
    w0 = inverse_factor(s0)
    l10 = dot_t(s1[:, :PW], w0)
    w1 = inverse_factor(s1[:, PW:] - dot_t(l10, l10))
    l20 = dot_t(s2[:, :PW], w0)
    l21 = dot_t(s2[:, PW : 2 * PW] - dot_t(l20, l10), w1)
    w2 = inverse_factor(s2[:, 2 * PW :] - dot_t(l20, l20) - dot_t(l21, l21))

    factors = panel_rows(panel, w0, w1, w2, l10, l20, l21)
    factors = jnp.concatenate(
        [jnp.where(row >= k, f, 0.0) for k, f in enumerate(factors)], axis=1
    )

    arrived = arrived.reshape(PW, width)
    own_rows = arrived[:, :head]
    rows = weave(own_rows, lax.ppermute(own_rows, "col", swap), col)
    k0, k1, k2 = panel_rows(rows, w0, w1, w2, l10, l20, l21)
    x2 = dot_n(k2, w2)
    x1 = dot_n(k1 - dot_n(x2, l21), w1)
    x0 = dot_n(k0 - dot_n(x1, l10) - dot_n(x2, l20), w0)
    x = jnp.concatenate([x0, x1, x2], axis=1)
    slots = jnp.arange(PW, dtype=jnp.int32)
    place = (arrived_index.reshape(1, PW) == slots[:, None]) & (slots[None, :] >= NP * CAP)
    place = place.astype(jnp.float32)
    update = lax.dot_general(
        dot_n(place, x),
        gathered,
        (((1,), (1,)), ((), ())),
        precision=lax.Precision.HIGH,
        preferred_element_type=jnp.float32,
    )
    column_ids = lax.broadcasted_iota(jnp.int32, (1, width), 1)
    parent = jnp.where(column_ids >= head, dot_n(place, arrived) - update, 0.0)
    return factors, parent


def solution(mesh):
    placed = (P("row", "col"), P("row", None))
    return jax.shard_map(
        local,
        mesh=mesh,
        in_specs=placed,
        out_specs=(P("row", None), P("row", "col")),
        check_vma=False,
    )
```

```python
import functools

import jax
import jax.numpy as jnp
from jax import lax
from jax.experimental import pallas as pl
from jax.experimental.pallas import tpu as pltpu
from jax.sharding import PartitionSpec as P

NP = 3
N_ROW = 64
CAP = 4
PW = 256
BW = 128
PANEL = NP * PW
HEAD = NP * BW
GRID = (4, 2, 4, 2)
PIECE_BLOCKS = (8, 8, 8, 4, 4)
PIECE_START = (0, 8, 16, 24, 28)

full = lax.Precision.HIGHEST


def dot_t(a, b):
    return lax.dot_general(
        a, b, (((1,), (1,)), ((), ())), precision=full, preferred_element_type=jnp.float32
    )


def dot_n(a, b):
    return lax.dot_general(
        a, b, (((1,), (0,)), ((), ())), precision=full, preferred_element_type=jnp.float32
    )


def row_id(z, y, x, k):
    return ((z * 2 + y) * 4 + x) * 2 + k


def pairs_of(kind, step):
    pairs = []
    for z in range(4):
        for y in range(2):
            for x in range(4):
                for k in range(2):
                    if kind == "y":
                        to = (z, 1 - y, x, k)
                    elif kind == "core":
                        to = (z, y, x, 1 - k)
                    elif (kind == "first") == (k == 0):
                        to = (z, y, (x + step) % 4, k)
                    else:
                        to = ((z + step) % 4, y, x, k)
                    pairs.append((row_id(z, y, x, k), row_id(*to)))
    return pairs


def move(value, kind, step=0):
    return lax.ppermute(value, "row", pairs_of(kind, step))


def ring(value, kind, beside=None):
    half = value.shape[0] // 2
    before = move(value, kind, 1)
    after = move(value, kind, -1)
    if beside is not None:
        before, after, beside = lax.optimization_barrier((before, after, beside))
    far_first = move(before[:half], kind, 1)
    far_second = move(after[half:], kind, -1)
    return [value, before, after, far_first, far_second], beside


def gather_rows(mine, beside):
    value = jnp.concatenate([mine, move(mine, "y")], axis=0)
    value = jnp.concatenate(ring(value, "first")[0], axis=0)
    pieces, beside = ring(value, "second", beside)
    return pieces + [move(p, "core") for p in pieces], beside


def block_order(row):
    z, y, x, k = row // 16, (row // 8) % 2, (row // 2) % 4, row % 2
    first = ((0, 0), (0, 1), (-1, 0), (-1, 1), (1, 0), (1, 1), (2, 0), (2, 1))
    order = []
    for swapped in (0, 1):
        core = k ^ swapped
        for second, part in ((0, first), (-1, first), (1, first), (2, first[:4]), (2, first[4:])):
            for along, flip in part:
                xs = jnp.where(core == 0, x + along, x + second) % 4
                zs = jnp.where(core == 0, z + second, z + along) % 4
                order.append(row_id(zs, y ^ flip, xs, core))
    return jnp.stack(order).astype(jnp.int32)


def pack_kernel(slot_ref, rows_ref, out_ref):
    for g in range(N_ROW):
        out_ref[slot_ref[g]] = rows_ref[g * CAP : (g + 1) * CAP, :]


def pack_runs(slots, rows, tile):
    height, width = rows.shape
    return pl.pallas_call(
        pack_kernel,
        out_shape=jax.ShapeDtypeStruct((N_ROW, CAP, width), rows.dtype),
        grid_spec=pltpu.PrefetchScalarGridSpec(
            num_scalar_prefetch=1,
            grid=(width // tile,),
            in_specs=[pl.BlockSpec((height, tile), lambda i, s: (0, i))],
            out_specs=pl.BlockSpec((N_ROW, CAP, tile), lambda i, s: (0, 0, i)),
        ),
        cost_estimate=pl.CostEstimate(
            flops=0, bytes_accessed=2 * 4 * height * width, transcendentals=0
        ),
        name="pack_runs",
    )(slots, rows)


def head_kernel(place_ref, col_ref, *refs):
    pieces, (rows_ref, square_ref), (sem,) = refs[:10], refs[10:12], refs[12:]
    for q in range(NP):
        at = place_ref[q]
        for p in range(10):
            low = 32 * (p // 5) + PIECE_START[p % 5]
            high = low + PIECE_BLOCKS[p % 5]

            @pl.when((at >= low) & (at < high))
            def _():
                start = pl.multiple_of((at - low) * BW, BW)
                copy = pltpu.make_async_copy(
                    pieces[p].at[pl.ds(start, BW)], rows_ref.at[pl.ds(q * BW, BW)], sem
                )
                copy.start()
                copy.wait()

    for c in range(2):

        @pl.when(col_ref[0] == c)
        def _():
            for q in range(NP):
                square_ref[:, q * BW : (q + 1) * BW] = rows_ref[
                    :, (2 * q + c) * BW : (2 * q + c + 1) * BW
                ]


def head_rows(place, col, pieces):
    return pl.pallas_call(
        head_kernel,
        out_shape=(
            jax.ShapeDtypeStruct((HEAD, PANEL), jnp.float32),
            jax.ShapeDtypeStruct((HEAD, HEAD), jnp.float32),
        ),
        in_specs=[pl.BlockSpec(memory_space=pltpu.SMEM)] * 2
        + [pl.BlockSpec(memory_space=pl.ANY)] * 10,
        out_specs=(pl.BlockSpec(memory_space=pltpu.VMEM),) * 2,
        scratch_shapes=[pltpu.SemaphoreType.DMA],
        cost_estimate=pl.CostEstimate(flops=0, bytes_accessed=4 * 10**6, transcendentals=0),
        name="head_rows",
    )(place, col, *pieces)


def inverse_lower(block, m):
    n = BW
    lane = lax.broadcasted_iota(jnp.int32, (8, n), 1)
    sub = lax.broadcasted_iota(jnp.int32, (8, n), 0)
    tiles = [block[8 * t : 8 * t + 8, :] for t in range(n // 8)]
    pivots = [None] * (n // 8)
    for k0 in range(0, n, m):
        tk, s0 = k0 // 8, k0 % 8
        group = (lane >= k0) & (lane < k0 + m)
        cols = [
            {
                t: jnp.broadcast_to(tiles[t][:, k0 + j : k0 + j + 1], (8, n))
                for t in range(tk, n // 8)
            }
            for j in range(m)
        ]
        rows, factors = [], []
        for j in range(m):
            unit = jnp.where(lane[:1] == k0 + j, 1.0, 0.0)
            r = jnp.where(group[:1], unit, tiles[tk][s0 + j : s0 + j + 1, :])
            for i in range(j):
                r = r - factors[i][tk][s0 + j : s0 + j + 1, :] * rows[i]
            rows.append(r)
            pivot = jnp.broadcast_to(cols[j][tk][s0 + j : s0 + j + 1, :], (8, n))
            kept = pivots[tk]
            pivots[tk] = pivot if kept is None else jnp.where(sub == s0 + j, pivot, kept)
            inverse = 1.0 / pivot
            f = {t: cols[j][t] * inverse for t in cols[j]}
            f[tk] = jnp.where(sub > s0 + j, f[tk], 0.0)
            factors.append(f)
            for l in range(j + 1, m):
                a = jnp.broadcast_to(cols[l][tk][s0 + j : s0 + j + 1, :], (8, n))
                for t in cols[l]:
                    cols[l][t] = cols[l][t] - f[t] * a
        rows = [jnp.broadcast_to(r, (8, n)) for r in rows]
        for t in range(tk, n // 8):
            if t == tk:
                unit = jnp.where(lane - k0 == sub - s0, 1.0, 0.0)
                v = jnp.where(group & (sub >= s0), unit, tiles[t])
            else:
                v = jnp.where(group, 0.0, tiles[t])
            for j in range(m):
                v = v - factors[j][t] * rows[j]
            tiles[t] = v
    out = [
        jnp.where(lane <= sub + 8 * t, tiles[t] * lax.rsqrt(pivots[t]), 0.0)
        for t in range(n // 8)
    ]
    return jnp.concatenate(out, axis=0)


def factor_kernel(col_ref, rows_ref, square_ref, w_ref):
    def span(i):
        return slice(i * BW, (i + 1) * BW)

    for c in range(2):

        @pl.when(col_ref[0] == c)
        def _():
            d = 1 - c
            for q in range(NP):
                for p in range(NP):
                    w_ref[span(2 * q + c), span(2 * p + c)] = rows_ref[span(q), span(2 * p + c)]
                    other = rows_ref[span(q), span(2 * p + d)]
                    w_ref[span(2 * q + c), span(2 * p + d)] = other
                    w_ref[span(2 * p + d), span(2 * q + c)] = other.T
                    w_ref[span(2 * q + d), span(2 * p + d)] = square_ref[span(q), span(p)]

    n = PANEL
    row_ids = lax.broadcasted_iota(jnp.int32, (n, BW), 0)
    eye = jnp.where(
        lax.broadcasted_iota(jnp.int32, (BW, BW), 0)
        == lax.broadcasted_iota(jnp.int32, (BW, BW), 1),
        1.0,
        0.0,
    )

    @pl.loop(0, n // BW)
    def _(b):
        at = pl.ds(pl.multiple_of(b * BW, BW), BW)
        inverse = inverse_lower(w_ref[at, at], 8)
        below = row_ids >= (b + 1) * BW
        column = jnp.where(below, w_ref[:, at], 0.0)
        lower = dot_t(column, inverse)
        w_ref[at, at] = eye
        r = dot_n(inverse, w_ref[at, :])
        w_ref[:, at] = jnp.where(below, 0.0, w_ref[:, at])
        w_ref[...] = w_ref[...] - dot_n(lower, r)
        w_ref[at, :] = r

    rows_of = lax.broadcasted_iota(jnp.int32, (n, n), 0)
    cols_of = lax.broadcasted_iota(jnp.int32, (n, n), 1)
    w_ref[...] = jnp.where(cols_of <= rows_of, w_ref[...], 0.0)


def inverse_factor(col, rows, square):
    return pl.pallas_call(
        factor_kernel,
        out_shape=jax.ShapeDtypeStruct((PANEL, PANEL), jnp.float32),
        in_specs=[pl.BlockSpec(memory_space=pltpu.SMEM)]
        + [pl.BlockSpec(memory_space=pltpu.VMEM)] * 2,
        out_specs=pl.BlockSpec(memory_space=pltpu.VMEM),
        compiler_params=pltpu.CompilerParams(vmem_limit_bytes=40 * 2**20),
        cost_estimate=pl.CostEstimate(
            flops=4 * 10**9, bytes_accessed=5 * 10**6, transcendentals=0
        ),
        name="inverse_factor",
    )(col, rows, square)


def update_kernel(order_ref, x_ref, *refs):
    pieces, out_ref = refs[:10], refs[10]
    high, low, held, made, in_sem, out_sem = refs[11:]
    steps = N_ROW // 2
    slots = held.shape[0]

    def fetch(step):
        for p in range(10):
            first = 16 * (p // 5) + PIECE_START[p % 5] // 2
            last = first + PIECE_BLOCKS[p % 5] // 2

            @pl.when((step >= first) & (step < last))
            def _():
                start = pl.multiple_of((step - first) * 2 * BW, 2 * BW)
                slot = lax.rem(step, slots)
                pltpu.make_async_copy(
                    pieces[p].at[pl.ds(start, 2 * BW)], held.at[slot], in_sem.at[slot]
                ).start()

    def store(step, half):
        slot = lax.rem(step, 2)
        to = pl.multiple_of(order_ref[2 * step + half] * BW, BW)
        return pltpu.make_async_copy(
            made.at[slot, half], out_ref.at[:, pl.ds(to, BW)], out_sem.at[slot, half]
        )

    for step in range(slots - 1):
        fetch(jnp.int32(step))
    x = x_ref[...]
    high[...] = x.astype(jnp.bfloat16)
    low[...] = (x - high[...].astype(jnp.float32)).astype(jnp.bfloat16)

    def times(a, b):
        return lax.dot_general(
            a, b, (((1,), (1,)), ((), ())), preferred_element_type=jnp.float32
        )

    @pl.loop(0, steps)
    def _(step):
        @pl.when(step + slots - 1 < steps)
        def _():
            fetch(step + slots - 1)

        slot = lax.rem(step, slots)
        pltpu.make_async_copy(
            pieces[0].at[pl.ds(0, 2 * BW)], held.at[slot], in_sem.at[slot]
        ).wait()
        rows = held[slot]
        rows_high = rows.astype(jnp.bfloat16)
        rows_low = (rows - rows_high.astype(jnp.float32)).astype(jnp.bfloat16)
        result = (
            times(high[...], rows_low) + times(low[...], rows_high)
        ) + times(high[...], rows_high)

        @pl.when(step >= 2)
        def _():
            for half in range(2):
                store(step - 2, half).wait()

        for half in range(2):
            made[lax.rem(step, 2), half] = result[:, half * BW : (half + 1) * BW]
            store(step, half).start()

    for step in range(steps - 2, steps):
        for half in range(2):
            store(jnp.int32(step), half).wait()


def update_of(order, x, pieces, width):
    return pl.pallas_call(
        update_kernel,
        out_shape=jax.ShapeDtypeStruct((PW, width), jnp.float32),
        in_specs=[pl.BlockSpec(memory_space=pltpu.SMEM), pl.BlockSpec(memory_space=pltpu.VMEM)]
        + [pl.BlockSpec(memory_space=pl.ANY)] * 10,
        out_specs=pl.BlockSpec(memory_space=pl.ANY),
        scratch_shapes=[
            pltpu.VMEM((PW, PANEL), jnp.bfloat16),
            pltpu.VMEM((PW, PANEL), jnp.bfloat16),
            pltpu.VMEM((4, 2 * BW, PANEL), jnp.float32),
            pltpu.VMEM((2, 2, PW, BW), jnp.float32),
            pltpu.SemaphoreType.DMA((4,)),
            pltpu.SemaphoreType.DMA((2, 2)),
        ],
        compiler_params=pltpu.CompilerParams(vmem_limit_bytes=40 * 2**20),
        cost_estimate=pl.CostEstimate(
            flops=6 * PW * width * PANEL, bytes_accessed=34 * 10**6, transcendentals=0
        ),
        name="update_of",
    )(order, x, *pieces)


def place_kernel(tile, place_ref, arrived_ref, update_ref, out_ref, rows):
    for b in range(N_ROW):
        rows[b * CAP : (b + 1) * CAP, :] = arrived_ref[b]
    place = place_ref[...]
    value = rows[...]
    total = None
    for part in range(3):
        piece = value.astype(jnp.bfloat16)
        term = jnp.dot(place, piece, preferred_element_type=jnp.float32)
        total = term if total is None else total + term
        if part < 2:
            value = value - piece.astype(jnp.float32)
    column = pl.program_id(0) * tile + lax.broadcasted_iota(jnp.int32, (1, tile), 1)
    out_ref[...] = jnp.where(column >= HEAD, total - update_ref[...], 0.0)


def place_rows(place, arrived, update, tile=512):
    width = arrived.shape[2]
    return pl.pallas_call(
        functools.partial(place_kernel, tile),
        out_shape=jax.ShapeDtypeStruct((PW, width), jnp.float32),
        grid=(width // tile,),
        in_specs=[
            pl.BlockSpec((PW, PW), lambda i: (0, 0)),
            pl.BlockSpec((N_ROW, CAP, tile), lambda i: (0, 0, i)),
            pl.BlockSpec((PW, tile), lambda i: (0, i)),
        ],
        out_specs=pl.BlockSpec((PW, tile), lambda i: (0, i)),
        scratch_shapes=[pltpu.VMEM((PW, tile), jnp.float32)],
        cost_estimate=pl.CostEstimate(
            flops=6 * PW * PW * width, bytes_accessed=12 * PW * width, transcendentals=0
        ),
        name="place_rows",
    )(place, arrived, update)


def weave(own, other, col):
    first = jnp.where(col == 0, own, other)
    second = jnp.where(col == 0, other, own)
    parts = []
    for k in range(NP):
        parts += [first[:, k * BW : (k + 1) * BW], second[:, k * BW : (k + 1) * BW]]
    return jnp.concatenate(parts, axis=1)


def local(front_matrix, row_map):
    width = front_matrix.shape[1]
    row = lax.axis_index("row")
    col = lax.axis_index("col")
    swap = [(0, 1), (1, 0)]
    own = front_matrix[:, :HEAD]
    panel = weave(own, lax.ppermute(own, "col", swap), col)

    targets = row_map[0].reshape(N_ROW, CAP)[:, 0] // PW
    within = (row_map[0] % PW).astype(jnp.float32)
    small = jnp.concatenate([panel, jnp.broadcast_to(within[:, None], (PW, BW))], axis=1)
    small = pack_runs(targets, small, small.shape[1])
    small = lax.all_to_all(small, "row", split_axis=0, concat_axis=0, tiled=True)
    outgoing = pack_runs(targets, front_matrix, 512)

    mine = lax.dynamic_slice_in_dim(panel, col * BW, BW, 0)
    pieces, small = gather_rows(mine, small)
    order = block_order(row)
    places = jnp.sum(
        jnp.where(
            order[None, :] == jnp.arange(NP, dtype=jnp.int32)[:, None],
            jnp.arange(N_ROW, dtype=jnp.int32)[None, :],
            0,
        ),
        axis=1,
    )
    cols = col.reshape(1).astype(jnp.int32)
    rows, square = head_rows(places, cols, pieces)
    other_square = lax.ppermute(square, "col", swap)
    outgoing, other_square = lax.optimization_barrier((outgoing, other_square))
    arrived = lax.all_to_all(outgoing, "row", split_axis=0, concat_axis=0, tiled=True)

    w = inverse_factor(cols, rows, other_square)
    small = small.reshape(PW, PANEL + BW)
    both = dot_t(jnp.concatenate([panel, small[:, :PANEL]], axis=0), w)
    panel_ids = lax.broadcasted_iota(jnp.int32, (1, PANEL), 1) // PW
    factors = jnp.where(row >= panel_ids, both[:PW], 0.0)

    slots = jnp.arange(PW, dtype=jnp.int32)
    goes = small[:, PANEL].astype(jnp.int32)
    place = (goes[None, :] == slots[:, None]) & (slots[None, :] >= NP * CAP)
    place = place.astype(jnp.float32)
    x = dot_n(dot_n(place, both[PW:]), w)
    update = update_of(order, x, pieces, width)
    parent = place_rows(place.astype(jnp.bfloat16), arrived, update)
    return factors, parent


def solution(mesh):
    placed = (P("row", "col"), P("row", None))
    return jax.shard_map(
        local,
        mesh=mesh,
        in_specs=placed,
        out_specs=(P("row", None), P("row", "col")),
        check_vma=False,
    )
```

```python
import functools

import jax
import jax.numpy as jnp
import numpy as np
from jax import lax
from jax.experimental import pallas as pl
from jax.experimental.pallas import tpu as pltpu
from jax.sharding import PartitionSpec as P

NP = 3
N_ROW = 64
CAP = 4
PW = 256
BW = 128
PANEL = NP * PW
HEAD = NP * BW
GRID = (4, 2, 4, 2)
PIECE_BLOCKS = (8, 8, 8, 4, 4)
PIECE_START = (0, 8, 16, 24, 28)

full = lax.Precision.HIGHEST


def dot_t(a, b):
    return lax.dot_general(
        a, b, (((1,), (1,)), ((), ())), precision=full, preferred_element_type=jnp.float32
    )


def dot_n(a, b):
    return lax.dot_general(
        a, b, (((1,), (0,)), ((), ())), precision=full, preferred_element_type=jnp.float32
    )


def row_id(z, y, x, k):
    return ((z * 2 + y) * 4 + x) * 2 + k


def pairs_of(kind, step):
    pairs = []
    for z in range(4):
        for y in range(2):
            for x in range(4):
                for k in range(2):
                    if kind == "y":
                        to = (z, 1 - y, x, k)
                    elif kind == "core":
                        to = (z, y, x, 1 - k)
                    elif (kind == "first") == (k == 0):
                        to = (z, y, (x + step) % 4, k)
                    else:
                        to = ((z + step) % 4, y, x, k)
                    pairs.append((row_id(z, y, x, k), row_id(*to)))
    return pairs


def move(value, kind, step=0):
    return lax.ppermute(value, "row", pairs_of(kind, step))


def ring(value, kind, beside):
    half = value.shape[0] // 2
    before = move(value, kind, 1)
    after = move(value, kind, -1)
    before, after, beside = lax.optimization_barrier((before, after, beside))
    far_first = move(before[:half], kind, 1)
    far_second = move(after[half:], kind, -1)
    return [value, before, after, far_first, far_second], beside


def gather_rows(mine, small, runs):
    value = jnp.concatenate([mine, move(mine, "y")], axis=0)
    parts, small = ring(value, "first", small)
    value = jnp.concatenate(parts, axis=0)
    pieces, runs = ring(value, "second", runs)
    runs, *swapped = lax.optimization_barrier((runs, *(move(p, "core") for p in pieces)))
    return pieces + swapped, small, runs


def block_table():
    first = ((0, 0), (0, 1), (-1, 0), (-1, 1), (1, 0), (1, 1), (2, 0), (2, 1))
    table = np.zeros((N_ROW, BW), np.int32)
    for row in range(N_ROW):
        z, y, x, k = row // 16, (row // 8) % 2, (row // 2) % 4, row % 2
        order = []
        for core in (k, 1 - k):
            for second, part in (
                (0, first), (-1, first), (1, first), (2, first[:4]), (2, first[4:])
            ):
                for along, flip in part:
                    xs, zs = (along, second) if core == 0 else (second, along)
                    order.append(row_id((z + zs) % 4, y ^ flip, (x + xs) % 4, core))
        table[row, :N_ROW] = order
        table[row, N_ROW : N_ROW + NP] = [order.index(q) for q in range(NP)]
    return table


def pack_kernel(slot_ref, rows_ref, out_ref):
    for g in range(N_ROW):
        out_ref[slot_ref[g]] = rows_ref[g * CAP : (g + 1) * CAP, :]


def pack_runs(slots, rows, start, width, tile):
    height = rows.shape[0]
    return pl.pallas_call(
        pack_kernel,
        out_shape=jax.ShapeDtypeStruct((N_ROW, CAP, width), rows.dtype),
        grid_spec=pltpu.PrefetchScalarGridSpec(
            num_scalar_prefetch=1,
            grid=(width // tile,),
            in_specs=[pl.BlockSpec((height, tile), lambda i, s: (0, i + start // tile))],
            out_specs=pl.BlockSpec((N_ROW, CAP, tile), lambda i, s: (0, 0, i)),
        ),
        cost_estimate=pl.CostEstimate(
            flops=0, bytes_accessed=2 * 4 * height * width, transcendentals=0
        ),
        name="pack_runs",
    )(slots, rows)


def head_kernel(place_ref, col_ref, *refs):
    pieces, (rows_ref, square_ref), (sem,) = refs[:10], refs[10:12], refs[12:]
    for q in range(NP):
        at = place_ref[q]
        for p in range(10):
            low = 32 * (p // 5) + PIECE_START[p % 5]
            high = low + PIECE_BLOCKS[p % 5]

            @pl.when((at >= low) & (at < high))
            def _():
                start = pl.multiple_of((at - low) * BW, BW)
                copy = pltpu.make_async_copy(
                    pieces[p].at[pl.ds(start, BW)], rows_ref.at[pl.ds(q * BW, BW)], sem
                )
                copy.start()
                copy.wait()

    for c in range(2):

        @pl.when(col_ref[0] == c)
        def _():
            for q in range(NP):
                square_ref[:, q * BW : (q + 1) * BW] = rows_ref[
                    :, (2 * q + c) * BW : (2 * q + c + 1) * BW
                ]


def head_rows(place, col, pieces):
    return pl.pallas_call(
        head_kernel,
        out_shape=(
            jax.ShapeDtypeStruct((HEAD, PANEL), jnp.float32),
            jax.ShapeDtypeStruct((HEAD, HEAD), jnp.float32),
        ),
        in_specs=[pl.BlockSpec(memory_space=pltpu.SMEM)] * 2
        + [pl.BlockSpec(memory_space=pl.ANY)] * 10,
        out_specs=(pl.BlockSpec(memory_space=pltpu.VMEM),) * 2,
        scratch_shapes=[pltpu.SemaphoreType.DMA],
        cost_estimate=pl.CostEstimate(flops=0, bytes_accessed=4 * 10**6, transcendentals=0),
        name="head_rows",
    )(place, col, *pieces)


def inverse_lower(block, m):
    n = BW
    lane = lax.broadcasted_iota(jnp.int32, (8, n), 1)
    sub = lax.broadcasted_iota(jnp.int32, (8, n), 0)
    tiles = [block[8 * t : 8 * t + 8, :] for t in range(n // 8)]
    pivots = [None] * (n // 8)
    for k0 in range(0, n, m):
        tk, s0 = k0 // 8, k0 % 8
        group = (lane >= k0) & (lane < k0 + m)
        cols = [
            {
                t: jnp.broadcast_to(tiles[t][:, k0 + j : k0 + j + 1], (8, n))
                for t in range(tk, n // 8)
            }
            for j in range(m)
        ]
        rows, factors = [], []
        for j in range(m):
            unit = jnp.where(lane[:1] == k0 + j, 1.0, 0.0)
            r = jnp.where(group[:1], unit, tiles[tk][s0 + j : s0 + j + 1, :])
            for i in range(j):
                r = r - factors[i][tk][s0 + j : s0 + j + 1, :] * rows[i]
            rows.append(r)
            pivot = jnp.broadcast_to(cols[j][tk][s0 + j : s0 + j + 1, :], (8, n))
            kept = pivots[tk]
            pivots[tk] = pivot if kept is None else jnp.where(sub == s0 + j, pivot, kept)
            inverse = 1.0 / pivot
            f = {t: cols[j][t] * inverse for t in cols[j]}
            f[tk] = jnp.where(sub > s0 + j, f[tk], 0.0)
            factors.append(f)
            for l in range(j + 1, m):
                a = jnp.broadcast_to(cols[l][tk][s0 + j : s0 + j + 1, :], (8, n))
                for t in cols[l]:
                    cols[l][t] = cols[l][t] - f[t] * a
        rows = [jnp.broadcast_to(r, (8, n)) for r in rows]
        for t in range(tk, n // 8):
            if t == tk:
                unit = jnp.where(lane - k0 == sub - s0, 1.0, 0.0)
                v = jnp.where(group & (sub >= s0), unit, tiles[t])
            else:
                v = jnp.where(group, 0.0, tiles[t])
            for j in range(m):
                v = v - factors[j][t] * rows[j]
            tiles[t] = v
    out = [
        jnp.where(lane <= sub + 8 * t, tiles[t] * lax.rsqrt(pivots[t]), 0.0)
        for t in range(n // 8)
    ]
    return jnp.concatenate(out, axis=0)


def factor_kernel(col_ref, rows_ref, squares_ref, w_ref):
    def span(i):
        return slice(i * BW, (i + 1) * BW)

    for c in range(2):

        @pl.when(col_ref[0] == c)
        def _():
            d = 1 - c
            for q in range(NP):
                for p in range(NP):
                    w_ref[span(2 * q + c), span(2 * p + c)] = rows_ref[span(q), span(2 * p + c)]
                    other = rows_ref[span(q), span(2 * p + d)]
                    w_ref[span(2 * q + c), span(2 * p + d)] = other
                    w_ref[span(2 * p + d), span(2 * q + c)] = other.T
                    square = squares_ref[span(NP * d + q), span(p)]
                    w_ref[span(2 * q + d), span(2 * p + d)] = square

    n = PANEL
    row_ids = lax.broadcasted_iota(jnp.int32, (n, BW), 0)
    eye = jnp.where(
        lax.broadcasted_iota(jnp.int32, (BW, BW), 0)
        == lax.broadcasted_iota(jnp.int32, (BW, BW), 1),
        1.0,
        0.0,
    )

    @pl.loop(0, n // BW)
    def _(b):
        at = pl.ds(pl.multiple_of(b * BW, BW), BW)
        inverse = inverse_lower(w_ref[at, at], 8)
        below = row_ids >= (b + 1) * BW
        column = jnp.where(below, w_ref[:, at], 0.0)
        lower = dot_t(column, inverse)
        w_ref[at, at] = eye
        r = dot_n(inverse, w_ref[at, :])
        w_ref[:, at] = jnp.where(below, 0.0, w_ref[:, at])
        w_ref[...] = w_ref[...] - dot_n(lower, r)
        w_ref[at, :] = r

    rows_of = lax.broadcasted_iota(jnp.int32, (n, n), 0)
    cols_of = lax.broadcasted_iota(jnp.int32, (n, n), 1)
    w_ref[...] = jnp.where(cols_of <= rows_of, w_ref[...], 0.0)


def inverse_factor(col, rows, squares):
    return pl.pallas_call(
        factor_kernel,
        out_shape=jax.ShapeDtypeStruct((PANEL, PANEL), jnp.float32),
        in_specs=[pl.BlockSpec(memory_space=pltpu.SMEM)]
        + [pl.BlockSpec(memory_space=pltpu.VMEM)] * 2,
        out_specs=pl.BlockSpec(memory_space=pltpu.VMEM),
        compiler_params=pltpu.CompilerParams(vmem_limit_bytes=40 * 2**20),
        cost_estimate=pl.CostEstimate(
            flops=4 * 10**9, bytes_accessed=5 * 10**6, transcendentals=0
        ),
        name="inverse_factor",
    )(col, rows, squares)


def update_kernel(order_ref, x_ref, *refs):
    pieces, out_ref = refs[:10], refs[10]
    high, low, held, made, in_sem, out_sem = refs[11:]
    steps = N_ROW // 2
    slots = held.shape[0]

    def fetch(step):
        for p in range(10):
            first = 16 * (p // 5) + PIECE_START[p % 5] // 2
            last = first + PIECE_BLOCKS[p % 5] // 2

            @pl.when((step >= first) & (step < last))
            def _():
                start = pl.multiple_of((step - first) * 2 * BW, 2 * BW)
                slot = lax.rem(step, slots)
                pltpu.make_async_copy(
                    pieces[p].at[pl.ds(start, 2 * BW)], held.at[slot], in_sem.at[slot]
                ).start()

    def store(step, half):
        slot = lax.rem(step, 2)
        to = pl.multiple_of(order_ref[2 * step + half] * BW, BW)
        return pltpu.make_async_copy(
            made.at[slot, half], out_ref.at[:, pl.ds(to, BW)], out_sem.at[slot, half]
        )

    for step in range(slots - 1):
        fetch(jnp.int32(step))
    x = x_ref[...]
    high[...] = x.astype(jnp.bfloat16)
    low[...] = (x - high[...].astype(jnp.float32)).astype(jnp.bfloat16)

    def times(a, b):
        return lax.dot_general(
            a, b, (((1,), (1,)), ((), ())), preferred_element_type=jnp.float32
        )

    @pl.loop(0, steps)
    def _(step):
        @pl.when(step + slots - 1 < steps)
        def _():
            fetch(step + slots - 1)

        slot = lax.rem(step, slots)
        pltpu.make_async_copy(
            pieces[0].at[pl.ds(0, 2 * BW)], held.at[slot], in_sem.at[slot]
        ).wait()
        rows = held[slot]
        rows_high = rows.astype(jnp.bfloat16)
        rows_low = (rows - rows_high.astype(jnp.float32)).astype(jnp.bfloat16)
        result = (
            times(high[...], rows_low) + times(low[...], rows_high)
        ) + times(high[...], rows_high)

        @pl.when(step >= 2)
        def _():
            for half in range(2):
                store(step - 2, half).wait()

        for half in range(2):
            made[lax.rem(step, 2), half] = result[:, half * BW : (half + 1) * BW]
            store(step, half).start()

    for step in range(steps - 2, steps):
        for half in range(2):
            store(jnp.int32(step), half).wait()


def update_of(order, x, pieces, width):
    return pl.pallas_call(
        update_kernel,
        out_shape=jax.ShapeDtypeStruct((PW, width), jnp.float32),
        in_specs=[pl.BlockSpec(memory_space=pltpu.SMEM), pl.BlockSpec(memory_space=pltpu.VMEM)]
        + [pl.BlockSpec(memory_space=pl.ANY)] * 10,
        out_specs=pl.BlockSpec(memory_space=pl.ANY),
        scratch_shapes=[
            pltpu.VMEM((PW, PANEL), jnp.bfloat16),
            pltpu.VMEM((PW, PANEL), jnp.bfloat16),
            pltpu.VMEM((4, 2 * BW, PANEL), jnp.float32),
            pltpu.VMEM((2, 2, PW, BW), jnp.float32),
            pltpu.SemaphoreType.DMA((4,)),
            pltpu.SemaphoreType.DMA((2, 2)),
        ],
        compiler_params=pltpu.CompilerParams(vmem_limit_bytes=40 * 2**20),
        cost_estimate=pl.CostEstimate(
            flops=6 * PW * width * PANEL, bytes_accessed=34 * 10**6, transcendentals=0
        ),
        name="update_of",
    )(order, x, *pieces)


def place_kernel(start, tile, goes_ref, arrived_ref, update_ref, *refs):
    out_ref = refs[-1]
    masked = start < HEAD
    if masked:
        column = pl.program_id(0) * tile + lax.broadcasted_iota(jnp.int32, (1, tile), 1)
        kept = column >= HEAD - start
    for b in range(N_ROW):
        for i in range(CAP):
            at = b * CAP + i
            if b < NP:
                value = jnp.zeros((1, tile), jnp.float32)
            else:
                value = arrived_ref[b, i : i + 1, :] - update_ref[at : at + 1, :]
                if masked:
                    value = jnp.where(kept, value, 0.0)
            out_ref[pl.ds(goes_ref[at], 1), :] = value


def place_rows(goes, arrived, update, start, parent=None, tile=512):
    width = arrived.shape[2]
    first = start // tile
    return pl.pallas_call(
        functools.partial(place_kernel, start, tile),
        out_shape=jax.ShapeDtypeStruct(update.shape, jnp.float32),
        grid=(width // tile,),
        in_specs=[
            pl.BlockSpec(memory_space=pltpu.SMEM),
            pl.BlockSpec((N_ROW, CAP, tile), lambda i: (0, 0, i)),
            pl.BlockSpec((PW, tile), lambda i: (0, i + first)),
        ]
        + ([] if parent is None else [pl.BlockSpec(memory_space=pl.ANY)]),
        out_specs=pl.BlockSpec((PW, tile), lambda i: (0, i + first)),
        input_output_aliases={} if parent is None else {3: 0},
        cost_estimate=pl.CostEstimate(
            flops=PW * width, bytes_accessed=12 * PW * width, transcendentals=0
        ),
        name="place_rows",
    )(goes, arrived, update, *([] if parent is None else [parent]))


def weave(own, other, col):
    first = jnp.where(col == 0, own, other)
    second = jnp.where(col == 0, other, own)
    parts = []
    for k in range(NP):
        parts += [first[:, k * BW : (k + 1) * BW], second[:, k * BW : (k + 1) * BW]]
    return jnp.concatenate(parts, axis=1)


def local(front_matrix, row_map):
    width = front_matrix.shape[1]
    row = lax.axis_index("row")
    col = lax.axis_index("col")
    swap = [(0, 1), (1, 0)]
    own = front_matrix[:, :HEAD]
    panel = weave(own, lax.ppermute(own, "col", swap), col)

    targets = row_map[0].reshape(N_ROW, CAP)[:, 0] // PW
    within = (row_map[0] % PW).astype(jnp.float32)
    small = jnp.concatenate([panel, jnp.broadcast_to(within[:, None], (PW, BW))], axis=1)
    small = pack_runs(targets, small, 0, PANEL + BW, PANEL + BW)
    mine = lax.dynamic_slice_in_dim(panel, col * BW, BW, 0)
    mine, small = lax.optimization_barrier((mine, small))
    small = lax.all_to_all(small, "row", split_axis=0, concat_axis=0, tiled=True)

    def packed(slots):
        return pack_runs(slots, front_matrix, 0, width, 512)

    def send(runs):
        return lax.all_to_all(runs, "row", split_axis=0, concat_axis=0, tiled=True)

    pieces, small, outgoing = gather_rows(mine, small, packed(targets))
    cuts = (0,)
    arrived = [send(outgoing)]

    table = lax.dynamic_slice_in_dim(jnp.asarray(block_table()), row, 1, 0)[0]
    order, places = table[:N_ROW], table[N_ROW : N_ROW + 8]
    cols = col.reshape(1).astype(jnp.int32)
    rows, square = head_rows(places, cols, pieces)
    squares = lax.all_gather(square, "col", axis=0, tiled=True)

    w = inverse_factor(cols, rows, squares)
    small = small.reshape(PW, PANEL + BW)
    goes = small[:, PANEL].astype(jnp.int32)
    lower = dot_t(small[:, :PANEL], w)
    update = update_of(order, dot_n(lower, w), pieces, width)
    panel_ids = lax.broadcasted_iota(jnp.int32, (1, PANEL), 1) // PW
    factors = jnp.where(row >= panel_ids, dot_t(panel, w), 0.0)
    parent = None
    for start, part in zip(cuts, arrived):
        parent = place_rows(goes, part, update, start, parent)
    return factors, parent


def solution(mesh):
    placed = (P("row", "col"), P("row", None))
    return jax.shard_map(
        local,
        mesh=mesh,
        in_specs=placed,
        out_specs=(P("row", None), P("row", "col")),
        check_vma=False,
    )
```

```python
import functools

import jax
import jax.numpy as jnp
import numpy as np
from jax import lax
from jax.experimental import pallas as pl
from jax.experimental.pallas import tpu as pltpu
from jax.sharding import PartitionSpec as P

NP = 3
N_ROW = 64
CAP = 4
PW = 256
BW = 128
PANEL = NP * PW
HEAD = NP * BW
GRID = (4, 2, 4, 2)
PIECE_BLOCKS = (8, 8, 8, 4, 4)
PIECE_START = (0, 8, 16, 24, 28)

full = lax.Precision.HIGHEST


def dot_t(a, b):
    return lax.dot_general(
        a, b, (((1,), (1,)), ((), ())), precision=full, preferred_element_type=jnp.float32
    )


def dot_n(a, b):
    return lax.dot_general(
        a, b, (((1,), (0,)), ((), ())), precision=full, preferred_element_type=jnp.float32
    )


def row_id(z, y, x, k):
    return ((z * 2 + y) * 4 + x) * 2 + k


def pairs_of(kind, step):
    pairs = []
    for z in range(4):
        for y in range(2):
            for x in range(4):
                for k in range(2):
                    if kind == "y":
                        to = (z, 1 - y, x, k)
                    elif kind == "core":
                        to = (z, y, x, 1 - k)
                    elif (kind == "first") == (k == 0):
                        to = (z, y, (x + step) % 4, k)
                    else:
                        to = ((z + step) % 4, y, x, k)
                    pairs.append((row_id(z, y, x, k), row_id(*to)))
    return pairs


def move(value, kind, step=0):
    return lax.ppermute(value, "row", pairs_of(kind, step))


def ring(value, kind, beside=None):
    half = value.shape[0] // 2
    before = move(value, kind, 1)
    after = move(value, kind, -1)
    if beside is not None:
        before, after, beside = lax.optimization_barrier((before, after, beside))
    far_first = move(before[:half], kind, 1)
    far_second = move(after[half:], kind, -1)
    return [value, before, after, far_first, far_second], beside


def gather_rows(value, runs):
    value = jnp.concatenate(ring(value, "first")[0], axis=0)
    pieces, runs = ring(value, "second", runs)
    return pieces + [move(p, "core") for p in pieces], runs


def block_table():
    first = ((0, 0), (0, 1), (-1, 0), (-1, 1), (1, 0), (1, 1), (2, 0), (2, 1))
    table = np.zeros((N_ROW, BW), np.int32)
    for row in range(N_ROW):
        z, y, x, k = row // 16, (row // 8) % 2, (row // 2) % 4, row % 2
        order = []
        for core in (k, 1 - k):
            for second, part in (
                (0, first), (-1, first), (1, first), (2, first[:4]), (2, first[4:])
            ):
                for along, flip in part:
                    xs, zs = (along, second) if core == 0 else (second, along)
                    order.append(row_id((z + zs) % 4, y ^ flip, (x + xs) % 4, core))
        table[row, :N_ROW] = order
        table[row, N_ROW : N_ROW + NP] = [order.index(q) for q in range(NP)]
    return table


def pack_kernel(slot_ref, rows_ref, out_ref):
    for g in range(N_ROW):
        out_ref[slot_ref[g]] = rows_ref[g * CAP : (g + 1) * CAP, :]


def pack_runs(slots, rows, start, width, tile):
    height = rows.shape[0]
    return pl.pallas_call(
        pack_kernel,
        out_shape=jax.ShapeDtypeStruct((N_ROW, CAP, width), rows.dtype),
        grid_spec=pltpu.PrefetchScalarGridSpec(
            num_scalar_prefetch=1,
            grid=(width // tile,),
            in_specs=[pl.BlockSpec((height, tile), lambda i, s: (0, i + start // tile))],
            out_specs=pl.BlockSpec((N_ROW, CAP, tile), lambda i, s: (0, 0, i)),
        ),
        cost_estimate=pl.CostEstimate(
            flops=0, bytes_accessed=2 * 4 * height * width, transcendentals=0
        ),
        name="pack_runs",
    )(slots, rows)


def head_kernel(place_ref, col_ref, *refs):
    pieces, (rows_ref, square_ref), (sems,) = refs[:10], refs[10:12], refs[12:]
    for q in range(NP):
        at = place_ref[q]
        for p in range(10):
            low = 32 * (p // 5) + PIECE_START[p % 5]
            high = low + PIECE_BLOCKS[p % 5]

            @pl.when((at >= low) & (at < high))
            def _():
                start = pl.multiple_of((at - low) * BW, BW)
                pltpu.make_async_copy(
                    pieces[p].at[pl.ds(start, BW)], rows_ref.at[pl.ds(q * BW, BW)], sems.at[q]
                ).start()

    for q in range(NP):
        pltpu.make_async_copy(
            pieces[0].at[pl.ds(0, BW)], rows_ref.at[pl.ds(q * BW, BW)], sems.at[q]
        ).wait()

    for c in range(2):

        @pl.when(col_ref[0] == c)
        def _():
            for q in range(NP):
                square_ref[:, q * BW : (q + 1) * BW] = rows_ref[
                    :, (2 * q + c) * BW : (2 * q + c + 1) * BW
                ]


def head_rows(place, col, pieces):
    return pl.pallas_call(
        head_kernel,
        out_shape=(
            jax.ShapeDtypeStruct((HEAD, PANEL), jnp.float32),
            jax.ShapeDtypeStruct((HEAD, HEAD), jnp.float32),
        ),
        in_specs=[pl.BlockSpec(memory_space=pltpu.SMEM)] * 2
        + [pl.BlockSpec(memory_space=pl.ANY)] * 10,
        out_specs=(pl.BlockSpec(memory_space=pltpu.VMEM),) * 2,
        scratch_shapes=[pltpu.SemaphoreType.DMA((NP,))],
        cost_estimate=pl.CostEstimate(flops=0, bytes_accessed=4 * 10**6, transcendentals=0),
        name="head_rows",
    )(place, col, *pieces)


def inverse_lower(block, m):
    n = BW
    lane = lax.broadcasted_iota(jnp.int32, (8, n), 1)
    sub = lax.broadcasted_iota(jnp.int32, (8, n), 0)
    tiles = [block[8 * t : 8 * t + 8, :] for t in range(n // 8)]
    pivots = [None] * (n // 8)
    for k0 in range(0, n, m):
        tk, s0 = k0 // 8, k0 % 8
        group = (lane >= k0) & (lane < k0 + m)
        cols = [
            {
                t: jnp.broadcast_to(tiles[t][:, k0 + j : k0 + j + 1], (8, n))
                for t in range(tk, n // 8)
            }
            for j in range(m)
        ]
        rows, factors = [], []
        for j in range(m):
            unit = jnp.where(lane[:1] == k0 + j, 1.0, 0.0)
            r = jnp.where(group[:1], unit, tiles[tk][s0 + j : s0 + j + 1, :])
            for i in range(j):
                r = r - factors[i][tk][s0 + j : s0 + j + 1, :] * rows[i]
            rows.append(r)
            pivot = jnp.broadcast_to(cols[j][tk][s0 + j : s0 + j + 1, :], (8, n))
            kept = pivots[tk]
            pivots[tk] = pivot if kept is None else jnp.where(sub == s0 + j, pivot, kept)
            inverse = 1.0 / pivot
            f = {t: cols[j][t] * inverse for t in cols[j]}
            f[tk] = jnp.where(sub > s0 + j, f[tk], 0.0)
            factors.append(f)
            for l in range(j + 1, m):
                a = jnp.broadcast_to(cols[l][tk][s0 + j : s0 + j + 1, :], (8, n))
                for t in cols[l]:
                    cols[l][t] = cols[l][t] - f[t] * a
        rows = [jnp.broadcast_to(r, (8, n)) for r in rows]
        for t in range(tk, n // 8):
            if t == tk:
                unit = jnp.where(lane - k0 == sub - s0, 1.0, 0.0)
                v = jnp.where(group & (sub >= s0), unit, tiles[t])
            else:
                v = jnp.where(group, 0.0, tiles[t])
            for j in range(m):
                v = v - factors[j][t] * rows[j]
            tiles[t] = v
    out = [
        jnp.where(lane <= sub + 8 * t, tiles[t] * lax.rsqrt(pivots[t]), 0.0)
        for t in range(n // 8)
    ]
    return jnp.concatenate(out, axis=0)


def factor_kernel(col_ref, rows_ref, square_ref, w_ref):
    def span(i):
        return slice(i * BW, (i + 1) * BW)

    for c in range(2):

        @pl.when(col_ref[0] == c)
        def _():
            d = 1 - c
            for q in range(NP):
                for p in range(NP):
                    w_ref[span(2 * q + c), span(2 * p + c)] = rows_ref[span(q), span(2 * p + c)]
                    other = rows_ref[span(q), span(2 * p + d)]
                    w_ref[span(2 * q + c), span(2 * p + d)] = other
                    w_ref[span(2 * p + d), span(2 * q + c)] = other.T
                    w_ref[span(2 * q + d), span(2 * p + d)] = square_ref[span(q), span(p)]

    n = PANEL
    row_ids = lax.broadcasted_iota(jnp.int32, (n, BW), 0)
    eye = jnp.where(
        lax.broadcasted_iota(jnp.int32, (BW, BW), 0)
        == lax.broadcasted_iota(jnp.int32, (BW, BW), 1),
        1.0,
        0.0,
    )

    @pl.loop(0, n // BW)
    def _(b):
        at = pl.ds(pl.multiple_of(b * BW, BW), BW)
        inverse = inverse_lower(w_ref[at, at], 8)
        below = row_ids >= (b + 1) * BW
        column = jnp.where(below, w_ref[:, at], 0.0)
        lower = dot_t(column, inverse)
        w_ref[at, at] = eye
        r = dot_n(inverse, w_ref[at, :])
        w_ref[:, at] = jnp.where(below, 0.0, w_ref[:, at])
        w_ref[...] = w_ref[...] - dot_n(lower, r)
        w_ref[at, :] = r

    rows_of = lax.broadcasted_iota(jnp.int32, (n, n), 0)
    cols_of = lax.broadcasted_iota(jnp.int32, (n, n), 1)
    w_ref[...] = jnp.where(cols_of <= rows_of, w_ref[...], 0.0)


def inverse_factor(col, rows, square):
    return pl.pallas_call(
        factor_kernel,
        out_shape=jax.ShapeDtypeStruct((PANEL, PANEL), jnp.float32),
        in_specs=[pl.BlockSpec(memory_space=pltpu.SMEM)]
        + [pl.BlockSpec(memory_space=pltpu.VMEM)] * 2,
        out_specs=pl.BlockSpec(memory_space=pltpu.VMEM),
        compiler_params=pltpu.CompilerParams(vmem_limit_bytes=40 * 2**20),
        cost_estimate=pl.CostEstimate(
            flops=4 * 10**9, bytes_accessed=5 * 10**6, transcendentals=0
        ),
        name="inverse_factor",
    )(col, rows, square)


def update_kernel(order_ref, x_ref, *refs):
    pieces, out_ref = refs[:10], refs[10]
    high, low, held, made, in_sem, out_sem = refs[11:]
    steps = N_ROW // 2
    slots = held.shape[0]

    def fetch(step):
        for p in range(10):
            first = 16 * (p // 5) + PIECE_START[p % 5] // 2
            last = first + PIECE_BLOCKS[p % 5] // 2

            @pl.when((step >= first) & (step < last))
            def _():
                start = pl.multiple_of((step - first) * 2 * BW, 2 * BW)
                slot = lax.rem(step, slots)
                pltpu.make_async_copy(
                    pieces[p].at[pl.ds(start, 2 * BW)], held.at[slot], in_sem.at[slot]
                ).start()

    def store(step, half):
        slot = lax.rem(step, 2)
        to = pl.multiple_of(order_ref[2 * step + half] * BW, BW)
        return pltpu.make_async_copy(
            made.at[slot, half], out_ref.at[:, pl.ds(to, BW)], out_sem.at[slot, half]
        )

    for step in range(slots - 1):
        fetch(jnp.int32(step))
    x = x_ref[...]
    high[...] = x.astype(jnp.bfloat16)
    low[...] = (x - high[...].astype(jnp.float32)).astype(jnp.bfloat16)

    def times(a, b):
        return lax.dot_general(
            a, b, (((1,), (1,)), ((), ())), preferred_element_type=jnp.float32
        )

    @pl.loop(0, steps)
    def _(step):
        @pl.when(step + slots - 1 < steps)
        def _():
            fetch(step + slots - 1)

        slot = lax.rem(step, slots)
        pltpu.make_async_copy(
            pieces[0].at[pl.ds(0, 2 * BW)], held.at[slot], in_sem.at[slot]
        ).wait()
        rows = held[slot]
        rows_high = rows.astype(jnp.bfloat16)
        rows_low = (rows - rows_high.astype(jnp.float32)).astype(jnp.bfloat16)
        result = (
            times(high[...], rows_low) + times(low[...], rows_high)
        ) + times(high[...], rows_high)

        @pl.when(step >= 2)
        def _():
            for half in range(2):
                store(step - 2, half).wait()

        for half in range(2):
            made[lax.rem(step, 2), half] = result[:, half * BW : (half + 1) * BW]
            store(step, half).start()

    for step in range(steps - 2, steps):
        for half in range(2):
            store(jnp.int32(step), half).wait()


def update_of(order, x, pieces, width):
    return pl.pallas_call(
        update_kernel,
        out_shape=jax.ShapeDtypeStruct((PW, width), jnp.float32),
        in_specs=[pl.BlockSpec(memory_space=pltpu.SMEM), pl.BlockSpec(memory_space=pltpu.VMEM)]
        + [pl.BlockSpec(memory_space=pl.ANY)] * 10,
        out_specs=pl.BlockSpec(memory_space=pl.ANY),
        scratch_shapes=[
            pltpu.VMEM((PW, PANEL), jnp.bfloat16),
            pltpu.VMEM((PW, PANEL), jnp.bfloat16),
            pltpu.VMEM((4, 2 * BW, PANEL), jnp.float32),
            pltpu.VMEM((2, 2, PW, BW), jnp.float32),
            pltpu.SemaphoreType.DMA((4,)),
            pltpu.SemaphoreType.DMA((2, 2)),
        ],
        compiler_params=pltpu.CompilerParams(vmem_limit_bytes=40 * 2**20),
        cost_estimate=pl.CostEstimate(
            flops=6 * PW * width * PANEL, bytes_accessed=34 * 10**6, transcendentals=0
        ),
        name="update_of",
    )(order, x, *pieces)


def place_kernel(tile, place_ref, arrived_ref, update_ref, out_ref, rows):
    rows[: NP * CAP, :] = jnp.zeros((NP * CAP, tile), jnp.float32)
    for b in range(NP, N_ROW):
        rows[b * CAP : (b + 1) * CAP, :] = arrived_ref[b]
    value = rows[...] - update_ref[...]
    high = value.astype(jnp.bfloat16)
    low = (value - high.astype(jnp.float32)).astype(jnp.bfloat16)
    place = place_ref[...]
    out_ref[...] = jnp.dot(place, low, preferred_element_type=jnp.float32) + jnp.dot(
        place, high, preferred_element_type=jnp.float32
    )

    @pl.when(pl.program_id(0) == 0)
    def _():
        out_ref[:, :HEAD] = jnp.zeros((PW, HEAD), jnp.float32)


def place_rows(place, arrived, update, tile=512):
    width = arrived.shape[2]
    return pl.pallas_call(
        functools.partial(place_kernel, tile),
        out_shape=jax.ShapeDtypeStruct((PW, width), jnp.float32),
        grid=(width // tile,),
        in_specs=[
            pl.BlockSpec((PW, PW), lambda i: (0, 0)),
            pl.BlockSpec((N_ROW, CAP, tile), lambda i: (0, 0, i)),
            pl.BlockSpec((PW, tile), lambda i: (0, i)),
        ],
        out_specs=pl.BlockSpec((PW, tile), lambda i: (0, i)),
        scratch_shapes=[pltpu.VMEM((PW, tile), jnp.float32)],
        cost_estimate=pl.CostEstimate(
            flops=4 * PW * PW * width, bytes_accessed=12 * PW * width, transcendentals=0
        ),
        name="place_rows",
    )(place, arrived, update)


def weave(own, other, col):
    first = jnp.where(col == 0, own, other)
    second = jnp.where(col == 0, other, own)
    parts = []
    for k in range(NP):
        parts += [first[:, k * BW : (k + 1) * BW], second[:, k * BW : (k + 1) * BW]]
    return jnp.concatenate(parts, axis=1)


def local(front_matrix, row_map):
    width = front_matrix.shape[1]
    row = lax.axis_index("row")
    col = lax.axis_index("col")
    swap = [(0, 1), (1, 0)]

    def send(runs):
        return lax.all_to_all(runs, "row", split_axis=0, concat_axis=0, tiled=True)

    def half_rows(half):
        return lax.dynamic_slice(front_matrix, (half * BW, 0), (BW, HEAD))

    own, others = half_rows(col), half_rows(1 - col)
    own_beside = lax.ppermute(others, "col", swap)
    own_across = move(own, "y")
    mine = weave(own, own_beside, col)
    across = weave(own_across, move(own_beside, "y"), col)
    others_beside = lax.ppermute(own, "col", swap)

    targets = row_map[0].reshape(N_ROW, CAP)[:, 0] // PW
    within = (row_map[0] % PW).astype(jnp.float32)
    outgoing = pack_runs(targets, front_matrix, 0, width, 512)
    pieces, outgoing = gather_rows(jnp.concatenate([mine, across], axis=0), outgoing)

    theirs = weave(others, others_beside, col)
    panel = jnp.concatenate(
        [jnp.where(col == 0, mine, theirs), jnp.where(col == 0, theirs, mine)], axis=0
    )
    small = jnp.concatenate([panel, jnp.broadcast_to(within[:, None], (PW, BW))], axis=1)
    small = pack_runs(targets, small, 0, PANEL + BW, PANEL + BW)

    table = lax.dynamic_slice_in_dim(jnp.asarray(block_table()), row, 1, 0)[0]
    order, places = table[:N_ROW], table[N_ROW : N_ROW + 8]
    cols = col.reshape(1).astype(jnp.int32)
    rows, square = head_rows(places, cols, pieces)
    square, small = lax.optimization_barrier((square, small))
    square = lax.ppermute(square, "col", swap)
    small = send(small)
    outgoing, square, small = lax.optimization_barrier((outgoing, square, small))
    arrived = send(outgoing)

    w = inverse_factor(cols, rows, square)
    small = small.reshape(PW, PANEL + BW)
    lower = dot_t(small[:, :PANEL], w)
    update = update_of(order, dot_n(lower, w), pieces, width)
    panel_ids = lax.broadcasted_iota(jnp.int32, (1, PANEL), 1) // PW
    factors = jnp.where(row >= panel_ids, dot_t(panel, w), 0.0)
    slots = jnp.arange(PW, dtype=jnp.int32)
    goes = small[:, PANEL].astype(jnp.int32)
    place = (goes[None, :] == slots[:, None]) & (slots[None, :] >= NP * CAP)
    return factors, place_rows(place.astype(jnp.bfloat16), arrived, update)


def solution(mesh):
    placed = (P("row", "col"), P("row", None))
    return jax.shard_map(
        local,
        mesh=mesh,
        in_specs=placed,
        out_specs=(P("row", None), P("row", "col")),
        check_vma=False,
    )
```

```python
import functools

import jax
import jax.numpy as jnp
import numpy as np
from jax import lax
from jax.experimental import pallas as pl
from jax.experimental.pallas import tpu as pltpu
from jax.sharding import PartitionSpec as P

NP = 3
N_ROW = 64
CAP = 4
PW = 256
BW = 128
PANEL = NP * PW
HEAD = NP * BW
PIECES = 16
PIECE = 4

LOWER = tuple((q, p) for q in range(NP) for p in range(q + 1))

full = lax.Precision.HIGHEST


def dot_t(a, b):
    return lax.dot_general(
        a, b, (((1,), (1,)), ((), ())), precision=full, preferred_element_type=jnp.float32
    )


def dot_n(a, b):
    return lax.dot_general(
        a, b, (((1,), (0,)), ((), ())), precision=full, preferred_element_type=jnp.float32
    )


def row_id(z, y, x, k):
    return ((z * 2 + y) * 4 + x) * 2 + k


def pairs_of(kind, step):
    pairs = []
    for z in range(4):
        for y in range(2):
            for x in range(4):
                for k in range(2):
                    if kind == "y":
                        to = (z, 1 - y, x, k)
                    elif kind == "core":
                        to = (z, y, x, 1 - k)
                    elif (kind == "first") == (k == 0):
                        to = (z, y, (x + step) % 4, k)
                    else:
                        to = ((z + step) % 4, y, x, k)
                    pairs.append((row_id(z, y, x, k), row_id(*to)))
    return pairs


def move(value, kind, step=0):
    return lax.ppermute(value, "row", pairs_of(kind, step))


def ring(near, across, kind, beside=None):
    before_near = move(near, kind, 1)
    after_across = move(across, kind, -1)
    before_across = move(across, kind, 1)
    after_near = move(near, kind, -1)
    if beside is not None:
        before_near, after_across, beside = lax.optimization_barrier(
            (before_near, after_across, beside)
        )
    far_near = move(before_near, kind, 1)
    far_across = move(after_across, kind, -1)
    return (
        [near, before_near, after_near, far_near],
        [across, before_across, after_across, far_across],
        beside,
    )


def gather_rows(mine, small, runs):
    near, across, small = ring(mine, move(mine, "y"), "first", small)
    near, across, runs = ring(
        jnp.concatenate(near, axis=0), jnp.concatenate(across, axis=0), "second", runs
    )
    pieces = near + across
    return pieces + [move(p, "core") for p in pieces], small, runs


def block_table():
    table = np.zeros((N_ROW, BW), np.int32)
    for row in range(N_ROW):
        z, y, x, k = row // 16, (row // 8) % 2, (row // 2) % 4, row % 2
        order = []
        for core in (k, 1 - k):
            for flip in (0, 1):
                for second in (0, -1, 1, 2):
                    for first in (0, -1, 1, 2):
                        xs, zs = (first, second) if core == 0 else (second, first)
                        order.append(row_id((z + zs) % 4, y ^ flip, (x + xs) % 4, core))
        table[row, :N_ROW] = order
        table[row, N_ROW : N_ROW + NP] = [order.index(q) for q in range(NP)]
    return table


def pack_kernel(slot_ref, rows_ref, out_ref):
    for g in range(N_ROW):
        out_ref[slot_ref[g]] = rows_ref[g * CAP : (g + 1) * CAP, :]


def pack_runs(slots, rows, start, width, tile):
    height = rows.shape[0]
    return pl.pallas_call(
        pack_kernel,
        out_shape=jax.ShapeDtypeStruct((N_ROW, CAP, width), rows.dtype),
        grid_spec=pltpu.PrefetchScalarGridSpec(
            num_scalar_prefetch=1,
            grid=(width // tile,),
            in_specs=[pl.BlockSpec((height, tile), lambda i, s: (0, i + start // tile))],
            out_specs=pl.BlockSpec((N_ROW, CAP, tile), lambda i, s: (0, 0, i)),
        ),
        cost_estimate=pl.CostEstimate(
            flops=0, bytes_accessed=2 * 4 * height * width, transcendentals=0
        ),
        name="pack_runs",
    )(slots, rows)


def head_kernel(place_ref, col_ref, *refs):
    pieces, (rows_ref, lower_ref), (sems,) = refs[:PIECES], refs[PIECES : PIECES + 2], refs[PIECES + 2 :]
    for q in range(NP):
        at = place_ref[q]
        for p in range(PIECES):

            @pl.when((at >= p * PIECE) & (at < (p + 1) * PIECE))
            def _():
                start = pl.multiple_of((at - p * PIECE) * BW, BW)
                pltpu.make_async_copy(
                    pieces[p].at[pl.ds(start, BW)], rows_ref.at[pl.ds(q * BW, BW)], sems.at[q]
                ).start()

    for q in range(NP):
        pltpu.make_async_copy(
            pieces[0].at[pl.ds(0, BW)], rows_ref.at[pl.ds(q * BW, BW)], sems.at[q]
        ).wait()

    for c in range(2):

        @pl.when(col_ref[0] == c)
        def _():
            for i, (q, p) in enumerate(LOWER):
                lower_ref[i * BW : (i + 1) * BW, :] = rows_ref[
                    q * BW : (q + 1) * BW, (2 * p + c) * BW : (2 * p + c + 1) * BW
                ]


def head_rows(place, col, pieces):
    return pl.pallas_call(
        head_kernel,
        out_shape=(
            jax.ShapeDtypeStruct((HEAD, PANEL), jnp.float32),
            jax.ShapeDtypeStruct((len(LOWER) * BW, BW), jnp.float32),
        ),
        in_specs=[pl.BlockSpec(memory_space=pltpu.SMEM)] * 2
        + [pl.BlockSpec(memory_space=pl.ANY)] * PIECES,
        out_specs=(pl.BlockSpec(memory_space=pltpu.VMEM),) * 2,
        scratch_shapes=[pltpu.SemaphoreType.DMA((NP,))],
        cost_estimate=pl.CostEstimate(flops=0, bytes_accessed=4 * 10**6, transcendentals=0),
        name="head_rows",
    )(place, col, *pieces)


def inverse_lower(block, m):
    n = BW
    lane = lax.broadcasted_iota(jnp.int32, (8, n), 1)
    sub = lax.broadcasted_iota(jnp.int32, (8, n), 0)
    tiles = [block[8 * t : 8 * t + 8, :] for t in range(n // 8)]
    pivots = [None] * (n // 8)
    for k0 in range(0, n, m):
        tk, s0 = k0 // 8, k0 % 8
        group = (lane >= k0) & (lane < k0 + m)
        cols = [
            {
                t: jnp.broadcast_to(tiles[t][:, k0 + j : k0 + j + 1], (8, n))
                for t in range(tk, n // 8)
            }
            for j in range(m)
        ]
        rows, factors = [], []
        for j in range(m):
            unit = jnp.where(lane[:1] == k0 + j, 1.0, 0.0)
            r = jnp.where(group[:1], unit, tiles[tk][s0 + j : s0 + j + 1, :])
            for i in range(j):
                r = r - factors[i][tk][s0 + j : s0 + j + 1, :] * rows[i]
            rows.append(r)
            pivot = jnp.broadcast_to(cols[j][tk][s0 + j : s0 + j + 1, :], (8, n))
            kept = pivots[tk]
            pivots[tk] = pivot if kept is None else jnp.where(sub == s0 + j, pivot, kept)
            inverse = 1.0 / pivot
            f = {t: cols[j][t] * inverse for t in cols[j]}
            f[tk] = jnp.where(sub > s0 + j, f[tk], 0.0)
            factors.append(f)
            for l in range(j + 1, m):
                a = jnp.broadcast_to(cols[l][tk][s0 + j : s0 + j + 1, :], (8, n))
                for t in cols[l]:
                    cols[l][t] = cols[l][t] - f[t] * a
        rows = [jnp.broadcast_to(r, (8, n)) for r in rows]
        for t in range(tk, n // 8):
            if t == tk:
                unit = jnp.where(lane - k0 == sub - s0, 1.0, 0.0)
                v = jnp.where(group & (sub >= s0), unit, tiles[t])
            else:
                v = jnp.where(group, 0.0, tiles[t])
            for j in range(m):
                v = v - factors[j][t] * rows[j]
            tiles[t] = v
    out = [
        jnp.where(lane <= sub + 8 * t, tiles[t] * lax.rsqrt(pivots[t]), 0.0)
        for t in range(n // 8)
    ]
    return jnp.concatenate(out, axis=0)


def factor_kernel(col_ref, rows_ref, lower_ref, w_ref):
    def span(i):
        return slice(i * BW, (i + 1) * BW)

    for c in range(2):

        @pl.when(col_ref[0] == c)
        def _():
            d = 1 - c
            for q in range(NP):
                for p in range(NP):
                    w_ref[span(2 * q + c), span(2 * p + c)] = rows_ref[span(q), span(2 * p + c)]
                    other = rows_ref[span(q), span(2 * p + d)]
                    w_ref[span(2 * q + c), span(2 * p + d)] = other
                    w_ref[span(2 * p + d), span(2 * q + c)] = other.T
            for i, (q, p) in enumerate(LOWER):
                block = lower_ref[span(i), :]
                w_ref[span(2 * q + d), span(2 * p + d)] = block
                if p < q:
                    w_ref[span(2 * p + d), span(2 * q + d)] = block.T

    n = PANEL
    row_ids = lax.broadcasted_iota(jnp.int32, (n, BW), 0)
    eye = jnp.where(
        lax.broadcasted_iota(jnp.int32, (BW, BW), 0)
        == lax.broadcasted_iota(jnp.int32, (BW, BW), 1),
        1.0,
        0.0,
    )

    @pl.loop(0, n // BW)
    def _(b):
        at = pl.ds(pl.multiple_of(b * BW, BW), BW)
        inverse = inverse_lower(w_ref[at, at], 8)
        below = row_ids >= (b + 1) * BW
        column = jnp.where(below, w_ref[:, at], 0.0)
        lower = dot_t(column, inverse)
        w_ref[at, at] = eye
        r = dot_n(inverse, w_ref[at, :])
        w_ref[:, at] = jnp.where(below, 0.0, w_ref[:, at])
        w_ref[...] = w_ref[...] - dot_n(lower, r)
        w_ref[at, :] = r

    rows_of = lax.broadcasted_iota(jnp.int32, (n, n), 0)
    cols_of = lax.broadcasted_iota(jnp.int32, (n, n), 1)
    w_ref[...] = jnp.where(cols_of <= rows_of, w_ref[...], 0.0)


def inverse_factor(col, rows, square):
    return pl.pallas_call(
        factor_kernel,
        out_shape=jax.ShapeDtypeStruct((PANEL, PANEL), jnp.float32),
        in_specs=[pl.BlockSpec(memory_space=pltpu.SMEM)]
        + [pl.BlockSpec(memory_space=pltpu.VMEM)] * 2,
        out_specs=pl.BlockSpec(memory_space=pltpu.VMEM),
        compiler_params=pltpu.CompilerParams(vmem_limit_bytes=40 * 2**20),
        cost_estimate=pl.CostEstimate(
            flops=4 * 10**9, bytes_accessed=5 * 10**6, transcendentals=0
        ),
        name="inverse_factor",
    )(col, rows, square)


def update_kernel(order_ref, x_ref, *refs):
    pieces, out_ref = refs[:PIECES], refs[PIECES]
    high, low, held, made, in_sem, out_sem = refs[PIECES + 1 :]
    steps = N_ROW // 2
    slots = held.shape[0]

    def fetch(step):
        for p in range(PIECES):
            first, last = p * PIECE // 2, (p + 1) * PIECE // 2

            @pl.when((step >= first) & (step < last))
            def _():
                start = pl.multiple_of((step - first) * 2 * BW, 2 * BW)
                slot = lax.rem(step, slots)
                pltpu.make_async_copy(
                    pieces[p].at[pl.ds(start, 2 * BW)], held.at[slot], in_sem.at[slot]
                ).start()

    def store(step, half):
        slot = lax.rem(step, 2)
        to = pl.multiple_of(order_ref[2 * step + half] * BW, BW)
        return pltpu.make_async_copy(
            made.at[slot, half], out_ref.at[:, pl.ds(to, BW)], out_sem.at[slot, half]
        )

    for step in range(slots - 1):
        fetch(jnp.int32(step))
    x = x_ref[...]
    high[...] = x.astype(jnp.bfloat16)
    low[...] = (x - high[...].astype(jnp.float32)).astype(jnp.bfloat16)

    def times(a, b):
        return lax.dot_general(
            a, b, (((1,), (1,)), ((), ())), preferred_element_type=jnp.float32
        )

    @pl.loop(0, steps)
    def _(step):
        @pl.when(step + slots - 1 < steps)
        def _():
            fetch(step + slots - 1)

        slot = lax.rem(step, slots)
        pltpu.make_async_copy(
            pieces[0].at[pl.ds(0, 2 * BW)], held.at[slot], in_sem.at[slot]
        ).wait()
        rows = held[slot]
        rows_high = rows.astype(jnp.bfloat16)
        rows_low = (rows - rows_high.astype(jnp.float32)).astype(jnp.bfloat16)
        result = (
            times(high[...], rows_low) + times(low[...], rows_high)
        ) + times(high[...], rows_high)

        @pl.when(step >= 2)
        def _():
            for half in range(2):
                store(step - 2, half).wait()

        for half in range(2):
            made[lax.rem(step, 2), half] = result[:, half * BW : (half + 1) * BW]
            store(step, half).start()

    for step in range(steps - 2, steps):
        for half in range(2):
            store(jnp.int32(step), half).wait()


def update_of(order, x, pieces, width):
    return pl.pallas_call(
        update_kernel,
        out_shape=jax.ShapeDtypeStruct((PW, width), jnp.float32),
        in_specs=[pl.BlockSpec(memory_space=pltpu.SMEM), pl.BlockSpec(memory_space=pltpu.VMEM)]
        + [pl.BlockSpec(memory_space=pl.ANY)] * PIECES,
        out_specs=pl.BlockSpec(memory_space=pl.ANY),
        scratch_shapes=[
            pltpu.VMEM((PW, PANEL), jnp.bfloat16),
            pltpu.VMEM((PW, PANEL), jnp.bfloat16),
            pltpu.VMEM((4, 2 * BW, PANEL), jnp.float32),
            pltpu.VMEM((2, 2, PW, BW), jnp.float32),
            pltpu.SemaphoreType.DMA((4,)),
            pltpu.SemaphoreType.DMA((2, 2)),
        ],
        compiler_params=pltpu.CompilerParams(vmem_limit_bytes=40 * 2**20),
        cost_estimate=pl.CostEstimate(
            flops=6 * PW * width * PANEL, bytes_accessed=34 * 10**6, transcendentals=0
        ),
        name="update_of",
    )(order, x, *pieces)


def place_kernel(tile, place_ref, arrived_ref, update_ref, out_ref, rows):
    rows[: NP * CAP, :] = jnp.zeros((NP * CAP, tile), jnp.float32)
    for b in range(NP, N_ROW):
        rows[b * CAP : (b + 1) * CAP, :] = arrived_ref[b]
    value = rows[...] - update_ref[...]
    high = value.astype(jnp.bfloat16)
    low = (value - high.astype(jnp.float32)).astype(jnp.bfloat16)
    place = place_ref[...]
    out_ref[...] = jnp.dot(place, low, preferred_element_type=jnp.float32) + jnp.dot(
        place, high, preferred_element_type=jnp.float32
    )

    @pl.when(pl.program_id(0) == 0)
    def _():
        out_ref[:, :HEAD] = jnp.zeros((PW, HEAD), jnp.float32)


def place_rows(place, arrived, update, tile=2048):
    width = arrived.shape[2]
    return pl.pallas_call(
        functools.partial(place_kernel, tile),
        out_shape=jax.ShapeDtypeStruct((PW, width), jnp.float32),
        grid=(width // tile,),
        in_specs=[
            pl.BlockSpec((PW, PW), lambda i: (0, 0)),
            pl.BlockSpec((N_ROW, CAP, tile), lambda i: (0, 0, i)),
            pl.BlockSpec((PW, tile), lambda i: (0, i)),
        ],
        out_specs=pl.BlockSpec((PW, tile), lambda i: (0, i)),
        scratch_shapes=[pltpu.VMEM((PW, tile), jnp.float32)],
        compiler_params=pltpu.CompilerParams(vmem_limit_bytes=40 * 2**20),
        cost_estimate=pl.CostEstimate(
            flops=4 * PW * PW * width, bytes_accessed=12 * PW * width, transcendentals=0
        ),
        name="place_rows",
    )(place, arrived, update)


def weave(own, other, col):
    first = jnp.where(col == 0, own, other)
    second = jnp.where(col == 0, other, own)
    parts = []
    for k in range(NP):
        parts += [first[:, k * BW : (k + 1) * BW], second[:, k * BW : (k + 1) * BW]]
    return jnp.concatenate(parts, axis=1)


def local(front_matrix, row_map):
    width = front_matrix.shape[1]
    row = lax.axis_index("row")
    col = lax.axis_index("col")
    swap = [(0, 1), (1, 0)]

    def send(runs):
        return lax.all_to_all(runs, "row", split_axis=0, concat_axis=0, tiled=True)

    def half_rows(half):
        return lax.dynamic_slice(front_matrix, (half * BW, 0), (BW, HEAD))

    own, others = half_rows(col), half_rows(1 - col)
    mine = weave(own, lax.ppermute(others, "col", swap), col)
    theirs = weave(others, lax.ppermute(own, "col", swap), col)
    panel = jnp.concatenate(
        [jnp.where(col == 0, mine, theirs), jnp.where(col == 0, theirs, mine)], axis=0
    )

    targets = row_map[0].reshape(N_ROW, CAP)[:, 0] // PW
    within = (row_map[0] % PW).astype(jnp.float32)
    small = jnp.concatenate([panel, jnp.broadcast_to(within[:, None], (PW, BW))], axis=1)
    small = send(pack_runs(targets, small, 0, PANEL + BW, PANEL + BW))
    outgoing = pack_runs(targets, front_matrix, 0, width, 512)
    pieces, small, outgoing = gather_rows(mine, small, outgoing)

    table = lax.dynamic_slice_in_dim(jnp.asarray(block_table()), row, 1, 0)[0]
    order, places = table[:N_ROW], table[N_ROW : N_ROW + 8]
    cols = col.reshape(1).astype(jnp.int32)
    rows, square = head_rows(places, cols, pieces)
    square = lax.ppermute(square, "col", swap)
    outgoing, square = lax.optimization_barrier((outgoing, square))
    arrived = send(outgoing)

    w = inverse_factor(cols, rows, square)
    small = small.reshape(PW, PANEL + BW)
    lower = dot_t(small[:, :PANEL], w)
    update = update_of(order, dot_n(lower, w), pieces, width)
    panel_ids = lax.broadcasted_iota(jnp.int32, (1, PANEL), 1) // PW
    factors = jnp.where(row >= panel_ids, dot_t(panel, w), 0.0)
    slots = jnp.arange(PW, dtype=jnp.int32)
    goes = small[:, PANEL].astype(jnp.int32)
    place = (goes[None, :] == slots[:, None]) & (slots[None, :] >= NP * CAP)
    return factors, place_rows(place.astype(jnp.bfloat16), arrived, update)


def solution(mesh):
    placed = (P("row", "col"), P("row", None))
    return jax.shard_map(
        local,
        mesh=mesh,
        in_specs=placed,
        out_specs=(P("row", None), P("row", "col")),
        check_vma=False,
    )
```

```python
import functools

import jax
import jax.numpy as jnp
import numpy as np
from jax import lax
from jax.experimental import pallas as pl
from jax.experimental.pallas import tpu as pltpu
from jax.sharding import PartitionSpec as P

NP = 3
N_ROW = 64
CAP = 4
PW = 256
BW = 128
PANEL = NP * PW
HEAD = NP * BW
PIECES = 16
PIECE = 4

LOWER = tuple((q, p) for q in range(NP) for p in range(q + 1))

full = lax.Precision.HIGHEST


def dot_t(a, b):
    return lax.dot_general(
        a, b, (((1,), (1,)), ((), ())), precision=full, preferred_element_type=jnp.float32
    )


def dot_n(a, b):
    return lax.dot_general(
        a, b, (((1,), (0,)), ((), ())), precision=full, preferred_element_type=jnp.float32
    )


def row_id(z, y, x, k):
    return ((z * 2 + y) * 4 + x) * 2 + k


def pairs_of(kind, step):
    pairs = []
    for z in range(4):
        for y in range(2):
            for x in range(4):
                for k in range(2):
                    if kind == "y":
                        to = (z, 1 - y, x, k)
                    elif kind == "core":
                        to = (z, y, x, 1 - k)
                    elif (kind == "first") == (k == 0):
                        to = (z, y, (x + step) % 4, k)
                    else:
                        to = ((z + step) % 4, y, x, k)
                    pairs.append((row_id(z, y, x, k), row_id(*to)))
    return pairs


def move(value, kind, step=0):
    return lax.ppermute(value, "row", pairs_of(kind, step))


def ring(near, across, kind, beside=None):
    before_near = move(near, kind, 1)
    after_across = move(across, kind, -1)
    before_across = move(across, kind, 1)
    after_near = move(near, kind, -1)
    if beside is not None:
        before_near, after_across, beside = lax.optimization_barrier(
            (before_near, after_across, beside)
        )
    far_near = move(before_near, kind, 1)
    far_across = move(after_across, kind, -1)
    far_near, far_across, before_across, after_near = lax.optimization_barrier(
        (far_near, far_across, before_across, after_near)
    )
    return (
        [near, before_near, after_near, far_near],
        [across, before_across, after_across, far_across],
        beside,
    )


def gather_rows(mine, small, runs):
    near, across, small = ring(mine, move(mine, "y"), "first", small)
    near, across, runs = lax.optimization_barrier(
        (jnp.concatenate(near, axis=0), jnp.concatenate(across, axis=0), runs)
    )
    near, across, _ = ring(near, across, "second")
    pieces = near + across
    runs, *swapped = lax.optimization_barrier((runs, *(move(p, "core") for p in pieces)))
    return pieces + swapped, small, runs


def block_table():
    table = np.zeros((N_ROW, BW), np.int32)
    for row in range(N_ROW):
        z, y, x, k = row // 16, (row // 8) % 2, (row // 2) % 4, row % 2
        order = []
        for core in (k, 1 - k):
            for flip in (0, 1):
                for second in (0, -1, 1, 2):
                    for first in (0, -1, 1, 2):
                        xs, zs = (first, second) if core == 0 else (second, first)
                        order.append(row_id((z + zs) % 4, y ^ flip, (x + xs) % 4, core))
        table[row, :N_ROW] = order
        table[row, N_ROW : N_ROW + NP] = [order.index(q) for q in range(NP)]
    return table


def pack_kernel(slot_ref, rows_ref, out_ref):
    for g in range(N_ROW):
        out_ref[slot_ref[g]] = rows_ref[g * CAP : (g + 1) * CAP, :]


def pack_runs(slots, rows, start, width, tile):
    height = rows.shape[0]
    return pl.pallas_call(
        pack_kernel,
        out_shape=jax.ShapeDtypeStruct((N_ROW, CAP, width), rows.dtype),
        grid_spec=pltpu.PrefetchScalarGridSpec(
            num_scalar_prefetch=1,
            grid=(width // tile,),
            in_specs=[pl.BlockSpec((height, tile), lambda i, s: (0, i + start // tile))],
            out_specs=pl.BlockSpec((N_ROW, CAP, tile), lambda i, s: (0, 0, i)),
        ),
        cost_estimate=pl.CostEstimate(
            flops=0, bytes_accessed=2 * 4 * height * width, transcendentals=0
        ),
        compiler_params=pltpu.CompilerParams(vmem_limit_bytes=60 * 2**20),
        name="pack_runs",
    )(slots, rows)


def head_kernel(place_ref, col_ref, *refs):
    pieces, (rows_ref, lower_ref), (sems,) = refs[:PIECES], refs[PIECES : PIECES + 2], refs[PIECES + 2 :]
    for q in range(NP):
        at = place_ref[q]
        for p in range(PIECES):

            @pl.when((at >= p * PIECE) & (at < (p + 1) * PIECE))
            def _():
                start = pl.multiple_of((at - p * PIECE) * BW, BW)
                pltpu.make_async_copy(
                    pieces[p].at[pl.ds(start, BW)], rows_ref.at[pl.ds(q * BW, BW)], sems.at[q]
                ).start()

    for q in range(NP):
        pltpu.make_async_copy(
            pieces[0].at[pl.ds(0, BW)], rows_ref.at[pl.ds(q * BW, BW)], sems.at[q]
        ).wait()

    for c in range(2):

        @pl.when(col_ref[0] == c)
        def _():
            for i, (q, p) in enumerate(LOWER):
                lower_ref[i * BW : (i + 1) * BW, :] = rows_ref[
                    q * BW : (q + 1) * BW, (2 * p + c) * BW : (2 * p + c + 1) * BW
                ]


def head_rows(place, col, pieces):
    return pl.pallas_call(
        head_kernel,
        out_shape=(
            jax.ShapeDtypeStruct((HEAD, PANEL), jnp.float32),
            jax.ShapeDtypeStruct((len(LOWER) * BW, BW), jnp.float32),
        ),
        in_specs=[pl.BlockSpec(memory_space=pltpu.SMEM)] * 2
        + [pl.BlockSpec(memory_space=pl.ANY)] * PIECES,
        out_specs=(pl.BlockSpec(memory_space=pltpu.VMEM),) * 2,
        scratch_shapes=[pltpu.SemaphoreType.DMA((NP,))],
        cost_estimate=pl.CostEstimate(flops=0, bytes_accessed=4 * 10**6, transcendentals=0),
        name="head_rows",
    )(place, col, *pieces)


def inverse_lower(block, m):
    n = BW
    lane = lax.broadcasted_iota(jnp.int32, (8, n), 1)
    sub = lax.broadcasted_iota(jnp.int32, (8, n), 0)
    tiles = [block[8 * t : 8 * t + 8, :] for t in range(n // 8)]
    pivots = [None] * (n // 8)
    for k0 in range(0, n, m):
        tk, s0 = k0 // 8, k0 % 8
        group = (lane >= k0) & (lane < k0 + m)
        cols = [
            {
                t: jnp.broadcast_to(tiles[t][:, k0 + j : k0 + j + 1], (8, n))
                for t in range(tk, n // 8)
            }
            for j in range(m)
        ]
        rows, factors = [], []
        for j in range(m):
            unit = jnp.where(lane[:1] == k0 + j, 1.0, 0.0)
            r = jnp.where(group[:1], unit, tiles[tk][s0 + j : s0 + j + 1, :])
            for i in range(j):
                r = r - factors[i][tk][s0 + j : s0 + j + 1, :] * rows[i]
            rows.append(r)
            pivot = jnp.broadcast_to(cols[j][tk][s0 + j : s0 + j + 1, :], (8, n))
            kept = pivots[tk]
            pivots[tk] = pivot if kept is None else jnp.where(sub == s0 + j, pivot, kept)
            inverse = 1.0 / pivot
            f = {t: cols[j][t] * inverse for t in cols[j]}
            f[tk] = jnp.where(sub > s0 + j, f[tk], 0.0)
            factors.append(f)
            for l in range(j + 1, m):
                a = jnp.broadcast_to(cols[l][tk][s0 + j : s0 + j + 1, :], (8, n))
                for t in cols[l]:
                    cols[l][t] = cols[l][t] - f[t] * a
        rows = [jnp.broadcast_to(r, (8, n)) for r in rows]
        for t in range(tk, n // 8):
            if t == tk:
                unit = jnp.where(lane - k0 == sub - s0, 1.0, 0.0)
                v = jnp.where(group & (sub >= s0), unit, tiles[t])
            else:
                v = jnp.where(group, 0.0, tiles[t])
            for j in range(m):
                v = v - factors[j][t] * rows[j]
            tiles[t] = v
    out = [
        jnp.where(lane <= sub + 8 * t, tiles[t] * lax.rsqrt(pivots[t]), 0.0)
        for t in range(n // 8)
    ]
    return jnp.concatenate(out, axis=0)


def factor_kernel(col_ref, rows_ref, lower_ref, w_ref):
    def span(i):
        return slice(i * BW, (i + 1) * BW)

    for c in range(2):

        @pl.when(col_ref[0] == c)
        def _():
            d = 1 - c
            for q in range(NP):
                for p in range(NP):
                    w_ref[span(2 * q + c), span(2 * p + c)] = rows_ref[span(q), span(2 * p + c)]
                    other = rows_ref[span(q), span(2 * p + d)]
                    w_ref[span(2 * q + c), span(2 * p + d)] = other
                    w_ref[span(2 * p + d), span(2 * q + c)] = other.T
            for i, (q, p) in enumerate(LOWER):
                block = lower_ref[span(i), :]
                w_ref[span(2 * q + d), span(2 * p + d)] = block
                if p < q:
                    w_ref[span(2 * p + d), span(2 * q + d)] = block.T

    n = PANEL
    row_ids = lax.broadcasted_iota(jnp.int32, (n, BW), 0)
    eye = jnp.where(
        lax.broadcasted_iota(jnp.int32, (BW, BW), 0)
        == lax.broadcasted_iota(jnp.int32, (BW, BW), 1),
        1.0,
        0.0,
    )

    @pl.loop(0, n // BW)
    def _(b):
        at = pl.ds(pl.multiple_of(b * BW, BW), BW)
        inverse = inverse_lower(w_ref[at, at], 8)
        below = row_ids >= (b + 1) * BW
        column = jnp.where(below, w_ref[:, at], 0.0)
        lower = dot_t(column, inverse)
        w_ref[at, at] = eye
        r = dot_n(inverse, w_ref[at, :])
        w_ref[:, at] = jnp.where(below, 0.0, w_ref[:, at])
        w_ref[...] = w_ref[...] - dot_n(lower, r)
        w_ref[at, :] = r

    rows_of = lax.broadcasted_iota(jnp.int32, (n, n), 0)
    cols_of = lax.broadcasted_iota(jnp.int32, (n, n), 1)
    w_ref[...] = jnp.where(cols_of <= rows_of, w_ref[...], 0.0)


def inverse_factor(col, rows, square):
    return pl.pallas_call(
        factor_kernel,
        out_shape=jax.ShapeDtypeStruct((PANEL, PANEL), jnp.float32),
        in_specs=[pl.BlockSpec(memory_space=pltpu.SMEM)]
        + [pl.BlockSpec(memory_space=pltpu.VMEM)] * 2,
        out_specs=pl.BlockSpec(memory_space=pltpu.VMEM),
        compiler_params=pltpu.CompilerParams(vmem_limit_bytes=60 * 2**20),
        cost_estimate=pl.CostEstimate(
            flops=2 * 10**11, bytes_accessed=5 * 10**6, transcendentals=0
        ),
        name="inverse_factor",
    )(col, rows, square)


def update_kernel(order_ref, x_ref, *refs):
    pieces, out_ref = refs[:PIECES], refs[PIECES]
    high, low, held, made, in_sem, out_sem = refs[PIECES + 1 :]
    steps = N_ROW // 2
    slots = held.shape[0]

    def fetch(step):
        for p in range(PIECES):
            first, last = p * PIECE // 2, (p + 1) * PIECE // 2

            @pl.when((step >= first) & (step < last))
            def _():
                start = pl.multiple_of((step - first) * 2 * BW, 2 * BW)
                slot = lax.rem(step, slots)
                pltpu.make_async_copy(
                    pieces[p].at[pl.ds(start, 2 * BW)], held.at[slot], in_sem.at[slot]
                ).start()

    def store(step, half):
        slot = lax.rem(step, 2)
        to = pl.multiple_of(order_ref[2 * step + half] * BW, BW)
        return pltpu.make_async_copy(
            made.at[slot, half], out_ref.at[:, pl.ds(to, BW)], out_sem.at[slot, half]
        )

    for step in range(slots - 1):
        fetch(jnp.int32(step))
    x = x_ref[...]
    high[...] = x.astype(jnp.bfloat16)
    low[...] = (x - high[...].astype(jnp.float32)).astype(jnp.bfloat16)

    def times(a, b):
        return lax.dot_general(
            a, b, (((1,), (1,)), ((), ())), preferred_element_type=jnp.float32
        )

    @pl.loop(0, steps)
    def _(step):
        @pl.when(step + slots - 1 < steps)
        def _():
            fetch(step + slots - 1)

        slot = lax.rem(step, slots)
        pltpu.make_async_copy(
            pieces[0].at[pl.ds(0, 2 * BW)], held.at[slot], in_sem.at[slot]
        ).wait()
        rows = held[slot]
        rows_high = rows.astype(jnp.bfloat16)
        rows_low = (rows - rows_high.astype(jnp.float32)).astype(jnp.bfloat16)
        result = (
            times(high[...], rows_low) + times(low[...], rows_high)
        ) + times(high[...], rows_high)

        @pl.when(step >= 2)
        def _():
            for half in range(2):
                store(step - 2, half).wait()

        for half in range(2):
            made[lax.rem(step, 2), half] = result[:, half * BW : (half + 1) * BW]
            store(step, half).start()

    for step in range(steps - 2, steps):
        for half in range(2):
            store(jnp.int32(step), half).wait()


def update_of(order, x, pieces, width):
    return pl.pallas_call(
        update_kernel,
        out_shape=jax.ShapeDtypeStruct((PW, width), jnp.float32),
        in_specs=[pl.BlockSpec(memory_space=pltpu.SMEM), pl.BlockSpec(memory_space=pltpu.VMEM)]
        + [pl.BlockSpec(memory_space=pl.ANY)] * PIECES,
        out_specs=pl.BlockSpec(memory_space=pl.ANY),
        scratch_shapes=[
            pltpu.VMEM((PW, PANEL), jnp.bfloat16),
            pltpu.VMEM((PW, PANEL), jnp.bfloat16),
            pltpu.VMEM((4, 2 * BW, PANEL), jnp.float32),
            pltpu.VMEM((2, 2, PW, BW), jnp.float32),
            pltpu.SemaphoreType.DMA((4,)),
            pltpu.SemaphoreType.DMA((2, 2)),
        ],
        compiler_params=pltpu.CompilerParams(vmem_limit_bytes=60 * 2**20),
        cost_estimate=pl.CostEstimate(
            flops=6 * PW * width * PANEL, bytes_accessed=34 * 10**6, transcendentals=0
        ),
        name="update_of",
    )(order, x, *pieces)


def place_kernel(tile, place_ref, arrived_ref, update_ref, out_ref, rows):
    rows[: NP * CAP, :] = jnp.zeros((NP * CAP, tile), jnp.float32)
    for b in range(NP, N_ROW):
        rows[b * CAP : (b + 1) * CAP, :] = arrived_ref[b]
    value = rows[...] - update_ref[...]
    high = value.astype(jnp.bfloat16)
    low = (value - high.astype(jnp.float32)).astype(jnp.bfloat16)
    place = place_ref[...]
    out_ref[...] = jnp.dot(place, low, preferred_element_type=jnp.float32) + jnp.dot(
        place, high, preferred_element_type=jnp.float32
    )

    @pl.when(pl.program_id(0) == 0)
    def _():
        out_ref[:, :HEAD] = jnp.zeros((PW, HEAD), jnp.float32)


def place_rows(place, arrived, update, tile=2048):
    width = arrived.shape[2]
    return pl.pallas_call(
        functools.partial(place_kernel, tile),
        out_shape=jax.ShapeDtypeStruct((PW, width), jnp.float32),
        grid=(width // tile,),
        in_specs=[
            pl.BlockSpec((PW, PW), lambda i: (0, 0)),
            pl.BlockSpec((N_ROW, CAP, tile), lambda i: (0, 0, i)),
            pl.BlockSpec((PW, tile), lambda i: (0, i)),
        ],
        out_specs=pl.BlockSpec((PW, tile), lambda i: (0, i)),
        scratch_shapes=[pltpu.VMEM((PW, tile), jnp.float32)],
        compiler_params=pltpu.CompilerParams(vmem_limit_bytes=60 * 2**20),
        cost_estimate=pl.CostEstimate(
            flops=4 * PW * PW * width, bytes_accessed=12 * PW * width, transcendentals=0
        ),
        name="place_rows",
    )(place, arrived, update)


def weave(own, other, col):
    first = jnp.where(col == 0, own, other)
    second = jnp.where(col == 0, other, own)
    parts = []
    for k in range(NP):
        parts += [first[:, k * BW : (k + 1) * BW], second[:, k * BW : (k + 1) * BW]]
    return jnp.concatenate(parts, axis=1)


def local(front_matrix, row_map):
    width = front_matrix.shape[1]
    row = lax.axis_index("row")
    col = lax.axis_index("col")
    swap = [(0, 1), (1, 0)]

    def send(runs):
        return lax.all_to_all(runs, "row", split_axis=0, concat_axis=0, tiled=True)

    def half_rows(half):
        return lax.dynamic_slice(front_matrix, (half * BW, 0), (BW, HEAD))

    own, others = half_rows(col), half_rows(1 - col)
    mine = weave(own, lax.ppermute(others, "col", swap), col)
    theirs = weave(others, lax.ppermute(own, "col", swap), col)
    panel = jnp.concatenate(
        [jnp.where(col == 0, mine, theirs), jnp.where(col == 0, theirs, mine)], axis=0
    )

    targets = row_map[0].reshape(N_ROW, CAP)[:, 0] // PW
    within = (row_map[0] % PW).astype(jnp.float32)
    small = jnp.concatenate(
        [front_matrix[:, :HEAD], jnp.broadcast_to(within[:, None], (PW, BW))], axis=1
    )
    small = send(pack_runs(targets, small, 0, HEAD + BW, HEAD + BW)).reshape(PW, HEAD + BW)
    outgoing = pack_runs(targets, front_matrix, 0, width, 2048)
    pieces, small, outgoing = gather_rows(mine, small, outgoing)

    table = lax.dynamic_slice_in_dim(jnp.asarray(block_table()), row, 1, 0)[0]
    order, places = table[:N_ROW], table[N_ROW : N_ROW + 8]
    cols = col.reshape(1).astype(jnp.int32)
    rows, square = head_rows(places, cols, pieces)
    sent_rows = small[:, :HEAD]
    panel_beside = lax.ppermute(sent_rows, "col", swap)
    square = lax.ppermute(square, "col", swap)
    outgoing, panel_beside, square = lax.optimization_barrier((outgoing, panel_beside, square))
    arrived = send(outgoing)

    w = inverse_factor(cols, rows, square)
    lower = dot_t(weave(sent_rows, panel_beside, col), w)
    update = update_of(order, dot_n(lower, w), pieces, width)
    panel_ids = lax.broadcasted_iota(jnp.int32, (1, PANEL), 1) // PW
    factors = jnp.where(row >= panel_ids, dot_t(panel, w), 0.0)
    slots = jnp.arange(PW, dtype=jnp.int32)
    goes = small[:, HEAD].astype(jnp.int32)
    place = (goes[None, :] == slots[:, None]) & (slots[None, :] >= NP * CAP)
    return factors, place_rows(place.astype(jnp.bfloat16), arrived, update)


def solution(mesh):
    placed = (P("row", "col"), P("row", None))
    return jax.shard_map(
        local,
        mesh=mesh,
        in_specs=placed,
        out_specs=(P("row", None), P("row", "col")),
        check_vma=False,
    )
```

```python
import functools

import jax
import jax.numpy as jnp
import numpy as np
from jax import lax
from jax.experimental import pallas as pl
from jax.experimental.pallas import tpu as pltpu
from jax.sharding import PartitionSpec as P

NP = 3
N_ROW = 64
CAP = 4
PW = 256
BW = 128
PANEL = NP * PW
HEAD = NP * BW
PIECES = 16
PIECE = 4

LOWER = tuple((q, p) for q in range(NP) for p in range(q + 1))

full = lax.Precision.HIGHEST


def dot_t(a, b):
    return lax.dot_general(
        a, b, (((1,), (1,)), ((), ())), precision=full, preferred_element_type=jnp.float32
    )


def dot_n(a, b):
    return lax.dot_general(
        a, b, (((1,), (0,)), ((), ())), precision=full, preferred_element_type=jnp.float32
    )


def row_id(z, y, x, k):
    return ((z * 2 + y) * 4 + x) * 2 + k


def pairs_of(kind, step):
    pairs = []
    for z in range(4):
        for y in range(2):
            for x in range(4):
                for k in range(2):
                    if kind == "y":
                        to = (z, 1 - y, x, k)
                    elif kind == "core":
                        to = (z, y, x, 1 - k)
                    elif (kind == "first") == (k == 0):
                        to = (z, y, (x + step) % 4, k)
                    else:
                        to = ((z + step) % 4, y, x, k)
                    pairs.append((row_id(z, y, x, k), row_id(*to)))
    return pairs


def move(value, kind, step=0):
    return lax.ppermute(value, "row", pairs_of(kind, step))


def ring(near, across, kind, beside=None):
    before_near = move(near, kind, 1)
    after_across = move(across, kind, -1)
    before_across = move(across, kind, 1)
    after_near = move(near, kind, -1)
    if beside is not None:
        before_near, after_across, beside = lax.optimization_barrier(
            (before_near, after_across, beside)
        )
    far_near = move(before_near, kind, 1)
    far_across = move(after_across, kind, -1)
    far_near, far_across, before_across, after_near = lax.optimization_barrier(
        (far_near, far_across, before_across, after_near)
    )
    return (
        [near, before_near, after_near, far_near],
        [across, before_across, after_across, far_across],
        beside,
    )


def block_table():
    table = np.zeros((N_ROW, BW), np.int32)
    for row in range(N_ROW):
        z, y, x, k = row // 16, (row // 8) % 2, (row // 2) % 4, row % 2
        order = []
        for core in (k, 1 - k):
            for flip in (0, 1):
                for second in (0, -1, 1, 2):
                    for first in (0, -1, 1, 2):
                        xs, zs = (first, second) if core == 0 else (second, first)
                        order.append(row_id((z + zs) % 4, y ^ flip, (x + xs) % 4, core))
        table[row, :N_ROW] = order
        table[row, N_ROW : N_ROW + NP] = [order.index(q) for q in range(NP)]
    return table


def pack_kernel(slot_ref, rows_ref, out_ref):
    for g in range(N_ROW):
        out_ref[slot_ref[g]] = rows_ref[g * CAP : (g + 1) * CAP, :]


def pack_runs(slots, rows, start, width, tile):
    height = rows.shape[0]
    return pl.pallas_call(
        pack_kernel,
        out_shape=jax.ShapeDtypeStruct((N_ROW, CAP, width), rows.dtype),
        grid_spec=pltpu.PrefetchScalarGridSpec(
            num_scalar_prefetch=1,
            grid=(width // tile,),
            in_specs=[pl.BlockSpec((height, tile), lambda i, s: (0, i + start // tile))],
            out_specs=pl.BlockSpec((N_ROW, CAP, tile), lambda i, s: (0, 0, i)),
        ),
        cost_estimate=pl.CostEstimate(
            flops=0, bytes_accessed=2 * 4 * height * width, transcendentals=0
        ),
        compiler_params=pltpu.CompilerParams(vmem_limit_bytes=60 * 2**20),
        name="pack_runs",
    )(slots, rows)


def head_kernel(place_ref, col_ref, *refs):
    pieces, (rows_ref, lower_ref), (sems,) = refs[:PIECES], refs[PIECES : PIECES + 2], refs[PIECES + 2 :]
    for q in range(NP):
        at = place_ref[q]
        for p in range(PIECES):

            @pl.when((at >= p * PIECE) & (at < (p + 1) * PIECE))
            def _():
                start = pl.multiple_of((at - p * PIECE) * BW, BW)
                pltpu.make_async_copy(
                    pieces[p].at[pl.ds(start, BW)], rows_ref.at[pl.ds(q * BW, BW)], sems.at[q]
                ).start()

    for q in range(NP):
        pltpu.make_async_copy(
            pieces[0].at[pl.ds(0, BW)], rows_ref.at[pl.ds(q * BW, BW)], sems.at[q]
        ).wait()

    for c in range(2):

        @pl.when(col_ref[0] == c)
        def _():
            for i, (q, p) in enumerate(LOWER):
                lower_ref[i * BW : (i + 1) * BW, :] = rows_ref[
                    q * BW : (q + 1) * BW, (2 * p + c) * BW : (2 * p + c + 1) * BW
                ]


def head_rows(place, col, pieces):
    return pl.pallas_call(
        head_kernel,
        out_shape=(
            jax.ShapeDtypeStruct((HEAD, PANEL), jnp.float32),
            jax.ShapeDtypeStruct((len(LOWER) * BW, BW), jnp.float32),
        ),
        in_specs=[pl.BlockSpec(memory_space=pltpu.SMEM)] * 2
        + [pl.BlockSpec(memory_space=pl.ANY)] * PIECES,
        out_specs=(pl.BlockSpec(memory_space=pltpu.VMEM),) * 2,
        scratch_shapes=[pltpu.SemaphoreType.DMA((NP,))],
        cost_estimate=pl.CostEstimate(flops=0, bytes_accessed=4 * 10**6, transcendentals=0),
        name="head_rows",
    )(place, col, *pieces)


def inverse_lower(block, m):
    n = BW
    lane = lax.broadcasted_iota(jnp.int32, (8, n), 1)
    sub = lax.broadcasted_iota(jnp.int32, (8, n), 0)
    tiles = [block[8 * t : 8 * t + 8, :] for t in range(n // 8)]
    pivots = [None] * (n // 8)
    for k0 in range(0, n, m):
        tk, s0 = k0 // 8, k0 % 8
        group = (lane >= k0) & (lane < k0 + m)
        cols = [
            {
                t: jnp.broadcast_to(tiles[t][:, k0 + j : k0 + j + 1], (8, n))
                for t in range(tk, n // 8)
            }
            for j in range(m)
        ]
        rows, factors = [], []
        for j in range(m):
            unit = jnp.where(lane[:1] == k0 + j, 1.0, 0.0)
            r = jnp.where(group[:1], unit, tiles[tk][s0 + j : s0 + j + 1, :])
            for i in range(j):
                r = r - factors[i][tk][s0 + j : s0 + j + 1, :] * rows[i]
            rows.append(r)
            pivot = jnp.broadcast_to(cols[j][tk][s0 + j : s0 + j + 1, :], (8, n))
            kept = pivots[tk]
            pivots[tk] = pivot if kept is None else jnp.where(sub == s0 + j, pivot, kept)
            inverse = 1.0 / pivot
            f = {t: cols[j][t] * inverse for t in cols[j]}
            f[tk] = jnp.where(sub > s0 + j, f[tk], 0.0)
            factors.append(f)
            for l in range(j + 1, m):
                a = jnp.broadcast_to(cols[l][tk][s0 + j : s0 + j + 1, :], (8, n))
                for t in cols[l]:
                    cols[l][t] = cols[l][t] - f[t] * a
        rows = [jnp.broadcast_to(r, (8, n)) for r in rows]
        for t in range(tk, n // 8):
            if t == tk:
                unit = jnp.where(lane - k0 == sub - s0, 1.0, 0.0)
                v = jnp.where(group & (sub >= s0), unit, tiles[t])
            else:
                v = jnp.where(group, 0.0, tiles[t])
            for j in range(m):
                v = v - factors[j][t] * rows[j]
            tiles[t] = v
    out = [
        jnp.where(lane <= sub + 8 * t, tiles[t] * lax.rsqrt(pivots[t]), 0.0)
        for t in range(n // 8)
    ]
    return jnp.concatenate(out, axis=0)


def factor_kernel(col_ref, rows_ref, lower_ref, w_ref):
    def span(i):
        return slice(i * BW, (i + 1) * BW)

    for c in range(2):

        @pl.when(col_ref[0] == c)
        def _():
            d = 1 - c
            for q in range(NP):
                for p in range(NP):
                    w_ref[span(2 * q + c), span(2 * p + c)] = rows_ref[span(q), span(2 * p + c)]
                    other = rows_ref[span(q), span(2 * p + d)]
                    w_ref[span(2 * q + c), span(2 * p + d)] = other
                    w_ref[span(2 * p + d), span(2 * q + c)] = other.T
            for i, (q, p) in enumerate(LOWER):
                block = lower_ref[span(i), :]
                w_ref[span(2 * q + d), span(2 * p + d)] = block
                if p < q:
                    w_ref[span(2 * p + d), span(2 * q + d)] = block.T

    n = PANEL
    row_ids = lax.broadcasted_iota(jnp.int32, (n, BW), 0)
    eye = jnp.where(
        lax.broadcasted_iota(jnp.int32, (BW, BW), 0)
        == lax.broadcasted_iota(jnp.int32, (BW, BW), 1),
        1.0,
        0.0,
    )

    @pl.loop(0, n // BW)
    def _(b):
        at = pl.ds(pl.multiple_of(b * BW, BW), BW)
        inverse = inverse_lower(w_ref[at, at], 8)
        below = row_ids >= (b + 1) * BW
        column = jnp.where(below, w_ref[:, at], 0.0)
        lower = dot_t(column, inverse)
        w_ref[at, at] = eye
        r = dot_n(inverse, w_ref[at, :])
        w_ref[:, at] = jnp.where(below, 0.0, w_ref[:, at])
        w_ref[...] = w_ref[...] - dot_n(lower, r)
        w_ref[at, :] = r

    rows_of = lax.broadcasted_iota(jnp.int32, (n, n), 0)
    cols_of = lax.broadcasted_iota(jnp.int32, (n, n), 1)
    w_ref[...] = jnp.where(cols_of <= rows_of, w_ref[...], 0.0)


def inverse_factor(col, rows, square):
    return pl.pallas_call(
        factor_kernel,
        out_shape=jax.ShapeDtypeStruct((PANEL, PANEL), jnp.float32),
        in_specs=[pl.BlockSpec(memory_space=pltpu.SMEM)]
        + [pl.BlockSpec(memory_space=pltpu.VMEM)] * 2,
        out_specs=pl.BlockSpec(memory_space=pltpu.VMEM),
        compiler_params=pltpu.CompilerParams(vmem_limit_bytes=60 * 2**20),
        cost_estimate=pl.CostEstimate(
            flops=2 * 10**11, bytes_accessed=5 * 10**6, transcendentals=0
        ),
        name="inverse_factor",
    )(col, rows, square)


def update_kernel(order_ref, x_ref, *refs):
    pieces, out_ref = refs[:PIECES], refs[PIECES]
    high, low, held, made, in_sem, out_sem = refs[PIECES + 1 :]
    steps = N_ROW // 2
    slots = held.shape[0]

    def fetch(step):
        for p in range(PIECES):
            first, last = p * PIECE // 2, (p + 1) * PIECE // 2

            @pl.when((step >= first) & (step < last))
            def _():
                start = pl.multiple_of((step - first) * 2 * BW, 2 * BW)
                slot = lax.rem(step, slots)
                pltpu.make_async_copy(
                    pieces[p].at[pl.ds(start, 2 * BW)], held.at[slot], in_sem.at[slot]
                ).start()

    def store(step, half):
        slot = lax.rem(step, 2)
        to = pl.multiple_of(order_ref[2 * step + half] * BW, BW)
        return pltpu.make_async_copy(
            made.at[slot, half], out_ref.at[:, pl.ds(to, BW)], out_sem.at[slot, half]
        )

    for step in range(slots - 1):
        fetch(jnp.int32(step))
    x = x_ref[...]
    high[...] = x.astype(jnp.bfloat16)
    low[...] = (x - high[...].astype(jnp.float32)).astype(jnp.bfloat16)

    def times(a, b):
        return lax.dot_general(
            a, b, (((1,), (1,)), ((), ())), preferred_element_type=jnp.float32
        )

    @pl.loop(0, steps)
    def _(step):
        @pl.when(step + slots - 1 < steps)
        def _():
            fetch(step + slots - 1)

        slot = lax.rem(step, slots)
        pltpu.make_async_copy(
            pieces[0].at[pl.ds(0, 2 * BW)], held.at[slot], in_sem.at[slot]
        ).wait()
        rows = held[slot]
        rows_high = rows.astype(jnp.bfloat16)
        rows_low = (rows - rows_high.astype(jnp.float32)).astype(jnp.bfloat16)
        result = (
            times(high[...], rows_low) + times(low[...], rows_high)
        ) + times(high[...], rows_high)

        @pl.when(step >= 2)
        def _():
            for half in range(2):
                store(step - 2, half).wait()

        for half in range(2):
            made[lax.rem(step, 2), half] = result[:, half * BW : (half + 1) * BW]
            store(step, half).start()

    for step in range(steps - 2, steps):
        for half in range(2):
            store(jnp.int32(step), half).wait()


def update_of(order, x, pieces, width):
    return pl.pallas_call(
        update_kernel,
        out_shape=jax.ShapeDtypeStruct((PW, width), jnp.float32),
        in_specs=[pl.BlockSpec(memory_space=pltpu.SMEM), pl.BlockSpec(memory_space=pltpu.VMEM)]
        + [pl.BlockSpec(memory_space=pl.ANY)] * PIECES,
        out_specs=pl.BlockSpec(memory_space=pl.ANY),
        scratch_shapes=[
            pltpu.VMEM((PW, PANEL), jnp.bfloat16),
            pltpu.VMEM((PW, PANEL), jnp.bfloat16),
            pltpu.VMEM((4, 2 * BW, PANEL), jnp.float32),
            pltpu.VMEM((2, 2, PW, BW), jnp.float32),
            pltpu.SemaphoreType.DMA((4,)),
            pltpu.SemaphoreType.DMA((2, 2)),
        ],
        compiler_params=pltpu.CompilerParams(vmem_limit_bytes=60 * 2**20),
        cost_estimate=pl.CostEstimate(
            flops=6 * PW * width * PANEL, bytes_accessed=34 * 10**6, transcendentals=0
        ),
        name="update_of",
    )(order, x, *pieces)


def place_kernel(tile, place_ref, arrived_ref, update_ref, out_ref, rows):
    rows[: NP * CAP, :] = jnp.zeros((NP * CAP, tile), jnp.float32)
    for b in range(NP, N_ROW):
        rows[b * CAP : (b + 1) * CAP, :] = arrived_ref[b]
    value = rows[...] - update_ref[...]
    high = value.astype(jnp.bfloat16)
    low = (value - high.astype(jnp.float32)).astype(jnp.bfloat16)
    place = place_ref[...]
    out_ref[...] = jnp.dot(place, low, preferred_element_type=jnp.float32) + jnp.dot(
        place, high, preferred_element_type=jnp.float32
    )

    @pl.when(pl.program_id(0) == 0)
    def _():
        out_ref[:, :HEAD] = jnp.zeros((PW, HEAD), jnp.float32)


def place_rows(place, arrived, update, tile=2048):
    width = arrived.shape[2]
    return pl.pallas_call(
        functools.partial(place_kernel, tile),
        out_shape=jax.ShapeDtypeStruct((PW, width), jnp.float32),
        grid=(width // tile,),
        in_specs=[
            pl.BlockSpec((PW, PW), lambda i: (0, 0)),
            pl.BlockSpec((N_ROW, CAP, tile), lambda i: (0, 0, i)),
            pl.BlockSpec((PW, tile), lambda i: (0, i)),
        ],
        out_specs=pl.BlockSpec((PW, tile), lambda i: (0, i)),
        scratch_shapes=[pltpu.VMEM((PW, tile), jnp.float32)],
        compiler_params=pltpu.CompilerParams(vmem_limit_bytes=60 * 2**20),
        cost_estimate=pl.CostEstimate(
            flops=4 * PW * PW * width, bytes_accessed=12 * PW * width, transcendentals=0
        ),
        name="place_rows",
    )(place, arrived, update)


def weave(own, other, col):
    first = jnp.where(col == 0, own, other)
    second = jnp.where(col == 0, other, own)
    parts = []
    for k in range(NP):
        parts += [first[:, k * BW : (k + 1) * BW], second[:, k * BW : (k + 1) * BW]]
    return jnp.concatenate(parts, axis=1)


def local(front_matrix, row_map):
    width = front_matrix.shape[1]
    row = lax.axis_index("row")
    col = lax.axis_index("col")
    swap = [(0, 1), (1, 0)]

    def send(runs):
        return lax.all_to_all(runs, "row", split_axis=0, concat_axis=0, tiled=True)

    def half_rows(half):
        return lax.dynamic_slice(front_matrix, (half * BW, 0), (BW, HEAD))

    own, others = half_rows(col), half_rows(1 - col)
    targets = row_map[0].reshape(N_ROW, CAP)[:, 0] // PW
    within = (row_map[0] % PW).astype(jnp.float32)
    small = jnp.concatenate(
        [front_matrix[:, :HEAD], jnp.broadcast_to(within[:, None], (PW, BW))], axis=1
    )
    small = pack_runs(targets, small, 0, HEAD + BW, HEAD + BW)
    own_beside, small = lax.optimization_barrier((lax.ppermute(others, "col", swap), small))
    mine = weave(own, own_beside, col)
    small = send(small)

    near, across, small = ring(mine, move(mine, "y"), "first", small)
    sent_rows, goes = small.reshape(PW, HEAD + BW)[:, :HEAD], small.reshape(PW, HEAD + BW)[:, HEAD]
    outgoing = pack_runs(targets, front_matrix, 0, width, 2048)
    near, across, outgoing, own = lax.optimization_barrier(
        (jnp.concatenate(near, axis=0), jnp.concatenate(across, axis=0), outgoing, own)
    )
    panel_beside = lax.ppermute(sent_rows, "col", swap)
    theirs = weave(others, lax.ppermute(own, "col", swap), col)
    near, across, _ = ring(near, across, "second")
    pieces = near + across
    pieces = pieces + [move(p, "core") for p in pieces]
    table = lax.dynamic_slice_in_dim(jnp.asarray(block_table()), row, 1, 0)[0]
    order, places = table[:N_ROW], table[N_ROW : N_ROW + 8]
    cols = col.reshape(1).astype(jnp.int32)
    rows, square = head_rows(places, cols, pieces)
    square = lax.ppermute(square, "col", swap)
    outgoing, square, panel_beside, theirs = lax.optimization_barrier(
        (outgoing, square, panel_beside, theirs)
    )
    arrived = send(outgoing)

    w = inverse_factor(cols, rows, square)
    panel = jnp.concatenate(
        [jnp.where(col == 0, mine, theirs), jnp.where(col == 0, theirs, mine)], axis=0
    )
    lower = dot_t(weave(sent_rows, panel_beside, col), w)
    update = update_of(order, dot_n(lower, w), pieces, width)
    panel_ids = lax.broadcasted_iota(jnp.int32, (1, PANEL), 1) // PW
    factors = jnp.where(row >= panel_ids, dot_t(panel, w), 0.0)
    slots = jnp.arange(PW, dtype=jnp.int32)
    goes = goes.astype(jnp.int32)
    place = (goes[None, :] == slots[:, None]) & (slots[None, :] >= NP * CAP)
    return factors, place_rows(place.astype(jnp.bfloat16), arrived, update)


def solution(mesh):
    placed = (P("row", "col"), P("row", None))
    return jax.shard_map(
        local,
        mesh=mesh,
        in_specs=placed,
        out_specs=(P("row", None), P("row", "col")),
        check_vma=False,
    )
```

```python
import functools

import jax
import jax.numpy as jnp
import numpy as np
from jax import lax
from jax.experimental import pallas as pl
from jax.experimental.pallas import tpu as pltpu
from jax.sharding import PartitionSpec as P

NP = 3
N_ROW = 64
CAP = 4
PW = 256
BW = 128
PANEL = NP * PW
HEAD = NP * BW
PIECES = 16
PIECE = 4

LOWER = tuple((q, p) for q in range(NP) for p in range(q + 1))

full = lax.Precision.HIGHEST


def dot_t(a, b):
    return lax.dot_general(
        a, b, (((1,), (1,)), ((), ())), precision=full, preferred_element_type=jnp.float32
    )


def dot_n(a, b):
    return lax.dot_general(
        a, b, (((1,), (0,)), ((), ())), precision=full, preferred_element_type=jnp.float32
    )


def row_id(z, y, x, k):
    return ((z * 2 + y) * 4 + x) * 2 + k


def pairs_of(kind, step):
    pairs = []
    for z in range(4):
        for y in range(2):
            for x in range(4):
                for k in range(2):
                    if kind == "y":
                        to = (z, 1 - y, x, k)
                    elif kind == "core":
                        to = (z, y, x, 1 - k)
                    elif (kind == "first") == (k == 0):
                        to = (z, y, (x + step) % 4, k)
                    else:
                        to = ((z + step) % 4, y, x, k)
                    pairs.append((row_id(z, y, x, k), row_id(*to)))
    return pairs


def move(value, kind, step=0):
    return lax.ppermute(value, "row", pairs_of(kind, step))


def ring(near, across, kind, beside=None):
    before_near = move(near, kind, 1)
    after_across = move(across, kind, -1)
    before_across = move(across, kind, 1)
    after_near = move(near, kind, -1)
    if beside is not None:
        before_near, after_across, beside = lax.optimization_barrier(
            (before_near, after_across, beside)
        )
    far_near = move(before_near, kind, 1)
    far_across = move(after_across, kind, -1)
    far_near, far_across, before_across, after_near = lax.optimization_barrier(
        (far_near, far_across, before_across, after_near)
    )
    return (
        [near, before_near, after_near, far_near],
        [across, before_across, after_across, far_across],
        beside,
    )


def block_table():
    table = np.zeros((N_ROW, BW), np.int32)
    for row in range(N_ROW):
        z, y, x, k = row // 16, (row // 8) % 2, (row // 2) % 4, row % 2
        order = []
        for core in (k, 1 - k):
            for flip in (0, 1):
                for second in (0, -1, 1, 2):
                    for first in (0, -1, 1, 2):
                        xs, zs = (first, second) if core == 0 else (second, first)
                        order.append(row_id((z + zs) % 4, y ^ flip, (x + xs) % 4, core))
        table[row, :N_ROW] = order
        table[row, N_ROW : N_ROW + NP] = [order.index(q) for q in range(NP)]
    return table


def pack_kernel(slot_ref, rows_ref, out_ref):
    for g in range(N_ROW):
        out_ref[slot_ref[g]] = rows_ref[g * CAP : (g + 1) * CAP, :]


def pack_runs(slots, rows, start, width, tile):
    height = rows.shape[0]
    return pl.pallas_call(
        pack_kernel,
        out_shape=jax.ShapeDtypeStruct((N_ROW, CAP, width), rows.dtype),
        grid_spec=pltpu.PrefetchScalarGridSpec(
            num_scalar_prefetch=1,
            grid=(width // tile,),
            in_specs=[pl.BlockSpec((height, tile), lambda i, s: (0, i + start // tile))],
            out_specs=pl.BlockSpec((N_ROW, CAP, tile), lambda i, s: (0, 0, i)),
        ),
        cost_estimate=pl.CostEstimate(
            flops=0, bytes_accessed=2 * 4 * height * width, transcendentals=0
        ),
        compiler_params=pltpu.CompilerParams(vmem_limit_bytes=60 * 2**20),
        name="pack_runs",
    )(slots, rows)


def head_kernel(place_ref, col_ref, *refs):
    pieces, (rows_ref, lower_ref), (sems,) = refs[:PIECES], refs[PIECES : PIECES + 2], refs[PIECES + 2 :]
    for q in range(NP):
        at = place_ref[q]
        for p in range(PIECES):

            @pl.when((at >= p * PIECE) & (at < (p + 1) * PIECE))
            def _():
                start = pl.multiple_of((at - p * PIECE) * BW, BW)
                pltpu.make_async_copy(
                    pieces[p].at[pl.ds(start, BW)], rows_ref.at[pl.ds(q * BW, BW)], sems.at[q]
                ).start()

    for q in range(NP):
        pltpu.make_async_copy(
            pieces[0].at[pl.ds(0, BW)], rows_ref.at[pl.ds(q * BW, BW)], sems.at[q]
        ).wait()

    for c in range(2):

        @pl.when(col_ref[0] == c)
        def _():
            for i, (q, p) in enumerate(LOWER):
                lower_ref[i * BW : (i + 1) * BW, :] = rows_ref[
                    q * BW : (q + 1) * BW, (2 * p + c) * BW : (2 * p + c + 1) * BW
                ]


def head_rows(place, col, pieces):
    return pl.pallas_call(
        head_kernel,
        out_shape=(
            jax.ShapeDtypeStruct((HEAD, PANEL), jnp.float32),
            jax.ShapeDtypeStruct((len(LOWER) * BW, BW), jnp.float32),
        ),
        in_specs=[pl.BlockSpec(memory_space=pltpu.SMEM)] * 2
        + [pl.BlockSpec(memory_space=pl.ANY)] * PIECES,
        out_specs=(pl.BlockSpec(memory_space=pltpu.VMEM),) * 2,
        scratch_shapes=[pltpu.SemaphoreType.DMA((NP,))],
        cost_estimate=pl.CostEstimate(flops=0, bytes_accessed=4 * 10**6, transcendentals=0),
        name="head_rows",
    )(place, col, *pieces)


def inverse_lower(block, m):
    n = BW
    lane = lax.broadcasted_iota(jnp.int32, (8, n), 1)
    sub = lax.broadcasted_iota(jnp.int32, (8, n), 0)
    tiles = [block[8 * t : 8 * t + 8, :] for t in range(n // 8)]
    pivots = [None] * (n // 8)
    for k0 in range(0, n, m):
        tk, s0 = k0 // 8, k0 % 8
        group = (lane >= k0) & (lane < k0 + m)
        cols = [
            {
                t: jnp.broadcast_to(tiles[t][:, k0 + j : k0 + j + 1], (8, n))
                for t in range(tk, n // 8)
            }
            for j in range(m)
        ]
        rows, factors = [], []
        for j in range(m):
            unit = jnp.where(lane[:1] == k0 + j, 1.0, 0.0)
            r = jnp.where(group[:1], unit, tiles[tk][s0 + j : s0 + j + 1, :])
            for i in range(j):
                r = r - factors[i][tk][s0 + j : s0 + j + 1, :] * rows[i]
            rows.append(r)
            pivot = jnp.broadcast_to(cols[j][tk][s0 + j : s0 + j + 1, :], (8, n))
            kept = pivots[tk]
            pivots[tk] = pivot if kept is None else jnp.where(sub == s0 + j, pivot, kept)
            inverse = 1.0 / pivot
            f = {t: cols[j][t] * inverse for t in cols[j]}
            f[tk] = jnp.where(sub > s0 + j, f[tk], 0.0)
            factors.append(f)
            for l in range(j + 1, m):
                a = jnp.broadcast_to(cols[l][tk][s0 + j : s0 + j + 1, :], (8, n))
                for t in cols[l]:
                    cols[l][t] = cols[l][t] - f[t] * a
        rows = [jnp.broadcast_to(r, (8, n)) for r in rows]
        for t in range(tk, n // 8):
            if t == tk:
                unit = jnp.where(lane - k0 == sub - s0, 1.0, 0.0)
                v = jnp.where(group & (sub >= s0), unit, tiles[t])
            else:
                v = jnp.where(group, 0.0, tiles[t])
            for j in range(m):
                v = v - factors[j][t] * rows[j]
            tiles[t] = v
    out = [
        jnp.where(lane <= sub + 8 * t, tiles[t] * lax.rsqrt(pivots[t]), 0.0)
        for t in range(n // 8)
    ]
    return jnp.concatenate(out, axis=0)


def factor_kernel(col_ref, rows_ref, lower_ref, w_ref):
    def span(i):
        return slice(i * BW, (i + 1) * BW)

    for c in range(2):

        @pl.when(col_ref[0] == c)
        def _():
            d = 1 - c
            for q in range(NP):
                for p in range(NP):
                    w_ref[span(2 * q + c), span(2 * p + c)] = rows_ref[span(q), span(2 * p + c)]
                    other = rows_ref[span(q), span(2 * p + d)]
                    w_ref[span(2 * q + c), span(2 * p + d)] = other
                    w_ref[span(2 * p + d), span(2 * q + c)] = other.T
            for i, (q, p) in enumerate(LOWER):
                block = lower_ref[span(i), :]
                w_ref[span(2 * q + d), span(2 * p + d)] = block
                if p < q:
                    w_ref[span(2 * p + d), span(2 * q + d)] = block.T

    n = PANEL
    row_ids = lax.broadcasted_iota(jnp.int32, (n, BW), 0)
    eye = jnp.where(
        lax.broadcasted_iota(jnp.int32, (BW, BW), 0)
        == lax.broadcasted_iota(jnp.int32, (BW, BW), 1),
        1.0,
        0.0,
    )

    @pl.loop(0, n // BW)
    def _(b):
        at = pl.ds(pl.multiple_of(b * BW, BW), BW)
        inverse = inverse_lower(w_ref[at, at], 8)
        below = row_ids >= (b + 1) * BW
        column = jnp.where(below, w_ref[:, at], 0.0)
        lower = dot_t(column, inverse)
        w_ref[at, at] = eye
        r = dot_n(inverse, w_ref[at, :])
        w_ref[:, at] = jnp.where(below, 0.0, w_ref[:, at])
        w_ref[...] = w_ref[...] - dot_n(lower, r)
        w_ref[at, :] = r

    rows_of = lax.broadcasted_iota(jnp.int32, (n, n), 0)
    cols_of = lax.broadcasted_iota(jnp.int32, (n, n), 1)
    w_ref[...] = jnp.where(cols_of <= rows_of, w_ref[...], 0.0)


def inverse_factor(col, rows, square):
    return pl.pallas_call(
        factor_kernel,
        out_shape=jax.ShapeDtypeStruct((PANEL, PANEL), jnp.float32),
        in_specs=[pl.BlockSpec(memory_space=pltpu.SMEM)]
        + [pl.BlockSpec(memory_space=pltpu.VMEM)] * 2,
        out_specs=pl.BlockSpec(memory_space=pltpu.VMEM),
        compiler_params=pltpu.CompilerParams(vmem_limit_bytes=60 * 2**20),
        cost_estimate=pl.CostEstimate(
            flops=2 * 10**11, bytes_accessed=5 * 10**6, transcendentals=0
        ),
        name="inverse_factor",
    )(col, rows, square)


def update_kernel(order_ref, x_ref, *refs):
    pieces, out_ref = refs[:PIECES], refs[PIECES]
    high, low, held, made, in_sem, out_sem = refs[PIECES + 1 :]
    steps = N_ROW // 2
    slots = held.shape[0]

    def fetch(step):
        for p in range(PIECES):
            first, last = p * PIECE // 2, (p + 1) * PIECE // 2

            @pl.when((step >= first) & (step < last))
            def _():
                start = pl.multiple_of((step - first) * 2 * BW, 2 * BW)
                slot = lax.rem(step, slots)
                pltpu.make_async_copy(
                    pieces[p].at[pl.ds(start, 2 * BW)], held.at[slot], in_sem.at[slot]
                ).start()

    def store(step, half):
        slot = lax.rem(step, 2)
        to = pl.multiple_of(order_ref[2 * step + half] * BW, BW)
        return pltpu.make_async_copy(
            made.at[slot, half], out_ref.at[:, pl.ds(to, BW)], out_sem.at[slot, half]
        )

    for step in range(slots - 1):
        fetch(jnp.int32(step))
    x = x_ref[...]
    high[...] = x.astype(jnp.bfloat16)
    low[...] = (x - high[...].astype(jnp.float32)).astype(jnp.bfloat16)

    def times(a, b):
        return lax.dot_general(
            a, b, (((1,), (1,)), ((), ())), preferred_element_type=jnp.float32
        )

    @pl.loop(0, steps)
    def _(step):
        @pl.when(step + slots - 1 < steps)
        def _():
            fetch(step + slots - 1)

        slot = lax.rem(step, slots)
        pltpu.make_async_copy(
            pieces[0].at[pl.ds(0, 2 * BW)], held.at[slot], in_sem.at[slot]
        ).wait()
        rows = held[slot]
        rows_high = rows.astype(jnp.bfloat16)
        rows_low = (rows - rows_high.astype(jnp.float32)).astype(jnp.bfloat16)
        result = (
            times(high[...], rows_low) + times(low[...], rows_high)
        ) + times(high[...], rows_high)

        @pl.when(step >= 2)
        def _():
            for half in range(2):
                store(step - 2, half).wait()

        for half in range(2):
            made[lax.rem(step, 2), half] = result[:, half * BW : (half + 1) * BW]
            store(step, half).start()

    for step in range(steps - 2, steps):
        for half in range(2):
            store(jnp.int32(step), half).wait()


def update_of(order, x, pieces, width):
    return pl.pallas_call(
        update_kernel,
        out_shape=jax.ShapeDtypeStruct((PW, width), jnp.float32),
        in_specs=[pl.BlockSpec(memory_space=pltpu.SMEM), pl.BlockSpec(memory_space=pltpu.VMEM)]
        + [pl.BlockSpec(memory_space=pl.ANY)] * PIECES,
        out_specs=pl.BlockSpec(memory_space=pl.ANY),
        scratch_shapes=[
            pltpu.VMEM((PW, PANEL), jnp.bfloat16),
            pltpu.VMEM((PW, PANEL), jnp.bfloat16),
            pltpu.VMEM((4, 2 * BW, PANEL), jnp.float32),
            pltpu.VMEM((2, 2, PW, BW), jnp.float32),
            pltpu.SemaphoreType.DMA((4,)),
            pltpu.SemaphoreType.DMA((2, 2)),
        ],
        compiler_params=pltpu.CompilerParams(vmem_limit_bytes=60 * 2**20),
        cost_estimate=pl.CostEstimate(
            flops=6 * PW * width * PANEL, bytes_accessed=34 * 10**6, transcendentals=0
        ),
        name="update_of",
    )(order, x, *pieces)


def place_kernel(tile, place_ref, arrived_ref, update_ref, out_ref, rows):
    rows[: NP * CAP, :] = jnp.zeros((NP * CAP, tile), jnp.float32)
    for b in range(NP, N_ROW):
        rows[b * CAP : (b + 1) * CAP, :] = arrived_ref[b]
    value = rows[...] - update_ref[...]
    high = value.astype(jnp.bfloat16)
    low = (value - high.astype(jnp.float32)).astype(jnp.bfloat16)
    place = place_ref[...]
    out_ref[...] = jnp.dot(place, low, preferred_element_type=jnp.float32) + jnp.dot(
        place, high, preferred_element_type=jnp.float32
    )

    @pl.when(pl.program_id(0) == 0)
    def _():
        out_ref[:, :HEAD] = jnp.zeros((PW, HEAD), jnp.float32)


def place_rows(place, arrived, update, tile=2048):
    width = arrived.shape[2]
    return pl.pallas_call(
        functools.partial(place_kernel, tile),
        out_shape=jax.ShapeDtypeStruct((PW, width), jnp.float32),
        grid=(width // tile,),
        in_specs=[
            pl.BlockSpec((PW, PW), lambda i: (0, 0)),
            pl.BlockSpec((N_ROW, CAP, tile), lambda i: (0, 0, i)),
            pl.BlockSpec((PW, tile), lambda i: (0, i)),
        ],
        out_specs=pl.BlockSpec((PW, tile), lambda i: (0, i)),
        scratch_shapes=[pltpu.VMEM((PW, tile), jnp.float32)],
        compiler_params=pltpu.CompilerParams(vmem_limit_bytes=60 * 2**20),
        cost_estimate=pl.CostEstimate(
            flops=4 * PW * PW * width, bytes_accessed=12 * PW * width, transcendentals=0
        ),
        name="place_rows",
    )(place, arrived, update)


def weave(own, other, col):
    first = jnp.where(col == 0, own, other)
    second = jnp.where(col == 0, other, own)
    parts = []
    for k in range(NP):
        parts += [first[:, k * BW : (k + 1) * BW], second[:, k * BW : (k + 1) * BW]]
    return jnp.concatenate(parts, axis=1)


def local(front_matrix, row_map):
    width = front_matrix.shape[1]
    row = lax.axis_index("row")
    col = lax.axis_index("col")
    swap = [(0, 1), (1, 0)]

    def send(runs):
        return lax.all_to_all(runs, "row", split_axis=0, concat_axis=0, tiled=True)

    def half_rows(half):
        return lax.dynamic_slice(front_matrix, (half * BW, 0), (BW, HEAD))

    own, others = half_rows(col), half_rows(1 - col)
    targets = row_map[0].reshape(N_ROW, CAP)[:, 0] // PW
    within = (row_map[0] % PW).astype(jnp.float32)
    small = jnp.concatenate(
        [front_matrix[:, :HEAD], jnp.broadcast_to(within[:, None], (PW, BW))], axis=1
    )
    small = pack_runs(targets, small, 0, HEAD + BW, HEAD + BW)
    own_beside, small = lax.optimization_barrier((lax.ppermute(others, "col", swap), small))
    mine = weave(own, own_beside, col)
    small = send(small)

    near, across, small = ring(mine, move(mine, "y"), "first", small)
    sent_rows, goes = small.reshape(PW, HEAD + BW)[:, :HEAD], small.reshape(PW, HEAD + BW)[:, HEAD]
    near, across, targets, own = lax.optimization_barrier(
        (jnp.concatenate(near, axis=0), jnp.concatenate(across, axis=0), targets, own)
    )
    outgoing = pack_runs(targets, front_matrix, 0, width, 2048)
    panel_beside = lax.ppermute(sent_rows, "col", swap)
    theirs = weave(others, lax.ppermute(own, "col", swap), col)
    near, across, _ = ring(near, across, "second")
    pieces = near + across
    pieces = pieces + [move(p, "core") for p in pieces]
    table = lax.dynamic_slice_in_dim(jnp.asarray(block_table()), row, 1, 0)[0]
    order, places = table[:N_ROW], table[N_ROW : N_ROW + 8]
    cols = col.reshape(1).astype(jnp.int32)
    rows, square = head_rows(places, cols, pieces)
    square = lax.ppermute(square, "col", swap)
    outgoing, square, panel_beside, theirs = lax.optimization_barrier(
        (outgoing, square, panel_beside, theirs)
    )
    arrived = send(outgoing)

    w = inverse_factor(cols, rows, square)
    panel = jnp.concatenate(
        [jnp.where(col == 0, mine, theirs), jnp.where(col == 0, theirs, mine)], axis=0
    )
    lower = dot_t(weave(sent_rows, panel_beside, col), w)
    update = update_of(order, dot_n(lower, w), pieces, width)
    panel_ids = lax.broadcasted_iota(jnp.int32, (1, PANEL), 1) // PW
    factors = jnp.where(row >= panel_ids, dot_t(panel, w), 0.0)
    slots = jnp.arange(PW, dtype=jnp.int32)
    goes = goes.astype(jnp.int32)
    place = (goes[None, :] == slots[:, None]) & (slots[None, :] >= NP * CAP)
    return factors, place_rows(place.astype(jnp.bfloat16), arrived, update)


def solution(mesh):
    placed = (P("row", "col"), P("row", None))
    return jax.shard_map(
        local,
        mesh=mesh,
        in_specs=placed,
        out_specs=(P("row", None), P("row", "col")),
        check_vma=False,
    )
```
